256 devices in a mesh: exp: 64 (over z, x, core), head: 4 (over y).
Axes of the slice: x: 4, y: 4, z: 8, core: 2. Of those that a mesh axis runs over, the one named last changes fastest.
Arguments:
- queries: bfloat16 [8192, 4096], P('exp', 'head')
- keys: bfloat16 [8192, 1024], P('exp', 'head')
- values: bfloat16 [8192, 1024], P('exp', 'head')
- w_in: bfloat16 [64, 4096, 2, 768], P('exp', 'head'), may hold values from -0.09375 to 0.09375
- w_out: bfloat16 [64, 768, 4096], P('exp', None, 'head'), may hold values from -0.21875 to 0.21875
- routes: int32 [8192, 6], P('exp'), may hold values from 0 to 63, as said below
- route_weights: float32 [8192, 6], P('exp'), may hold values from 0.05 to 0.45
- grad_out: bfloat16 [8192, 4096], P('exp', 'head'), may hold values from -6 to 6
Outputs:
- output: bfloat16 [8192, 4096], P('exp', 'head')
- grad_attended: bfloat16 [8192, 4096], P('exp', 'head')
The draws below stay inside these ranges and needn't reach their ends.
Inputs may be any that keep to these rules, and one draw needn't show every extreme that they name: `routes`: each row names 6 different experts. In each aligned block of 128 rows (the rows of one index of exp) no expert is named more than 14 times.
All inputs are finite; a program needn't handle non-finite values.
Results may differ from the reference program's by a relative error of at most 0.017.
Values may be sent and summed in bfloat16 or wider, within the bound.
No kernel may reach another device: no remote copies, remote signals or barrier semaphores. Data moves between devices by JAX's collectives and lax.ppermute only.
A program may use at most 128 MiB of HBM per device.

```python
import jax
import jax.numpy as jnp
from jax import lax

D = 4096
QUERY_HEADS = 32
KEY_VALUE_HEADS = 8
HEAD_WIDTH = 128
FF = 768
TOP = 6
TOK_DEV = 128
CACHE_PER_INDEX = 128
EXPERTS = 64
WINDOW_TOKENS = 8192
CACHE_POSITIONS = 8192
MEAN_LOAD = 12
CAP = 14


def drawn_keys(key):
    return 1.5 * jax.random.truncated_normal(jax.random.fold_in(key, 11), -4.0, 4.0, (CACHE_POSITIONS, KEY_VALUE_HEADS * HEAD_WIDTH), jnp.float32)


def draw_keys(key, part):
    starting_key_rows = drawn_keys(key)
    return starting_key_rows.astype(jnp.bfloat16)


def draw_queries(key, part):
    unrouted = 1.5 * jax.random.truncated_normal(jax.random.fold_in(key, 13), -4.0, 4.0, (WINDOW_TOKENS, QUERY_HEADS * HEAD_WIDTH), jnp.float32)
    return unrouted.astype(jnp.bfloat16)


def draw_values(key, part):
    unrouted = jax.random.truncated_normal(jax.random.fold_in(key, 17), -4.0, 4.0, (CACHE_POSITIONS, KEY_VALUE_HEADS * HEAD_WIDTH), jnp.float32)
    return unrouted.astype(jnp.bfloat16)


def draw_routes(key, part):
    block_total = WINDOW_TOKENS // TOK_DEV
    spread = CAP - MEAN_LOAD
    order = jax.random.permutation(jax.random.fold_in(key, 21), EXPERTS)

    def one_block(block_key):
        offsets = jax.random.randint(jax.random.fold_in(block_key, 1), (EXPERTS // 2,), 0, spread + 1)
        offsets = offsets.at[0].set(spread)
        signed = jnp.stack([offsets, -offsets], axis=1).reshape(EXPERTS)
        counts = jnp.zeros((EXPERTS,), jnp.int32).at[order].set(MEAN_LOAD + signed)
        ends = jnp.cumsum(counts)
        positions = jnp.arange(TOK_DEV * TOP, dtype=jnp.int32)
        listing = jnp.sum((ends[None, :] <= positions[:, None]).astype(jnp.int32), axis=1)
        table = listing.reshape(TOP, TOK_DEV).T
        ranks = jax.random.randint(jax.random.fold_in(block_key, 3), (TOK_DEV, TOP), 0, 1000) * TOP
        ranks = ranks + jnp.arange(TOP, dtype=jnp.int32)[None, :]
        column_order = jnp.argsort(ranks, axis=1, stable=True)
        table = jnp.take_along_axis(table, column_order, axis=1)
        shuffle = jax.random.permutation(jax.random.fold_in(block_key, 2), TOK_DEV)
        return table[shuffle]
    block_keys = jax.random.split(jax.random.fold_in(key, 22), block_total)
    return jax.vmap(one_block)(block_keys).reshape(WINDOW_TOKENS, TOP).astype(jnp.int32)


def block_levels(own_key, dims, cuts, least, top_value):
    loudness, own = 1.0, jax.random.fold_in(own_key, 6)
    for dim, shards_of in cuts:
        draws = jnp.exp(jax.random.uniform(jax.random.fold_in(own, dim), (shards_of,), jnp.float32, least / len(cuts), top_value / len(cuts)))
        loudness = loudness * jnp.repeat(draws, dims[dim] // shards_of).reshape([-1 if axis == dim else 1 for axis in range(len(dims))])
    return loudness


def normal_values(rng, shape, width, bound, cuts=(), kind=jnp.bfloat16):
    result = jax.random.normal(rng, shape, jnp.float32) * width
    if len(cuts) > 0:
        result = block_levels(rng, shape, cuts, -0.22, 0.18) * result
    return jnp.clip(result, min=-bound, max=bound).astype(kind)


def setup_inputs(seed: int = 0) -> dict:
    key_of = jax.random.split(jax.random.key(seed), 9)
    return {
        "queries": draw_queries(jax.random.fold_in(key_of[8], 71), 0),
        "keys": draw_keys(jax.random.fold_in(key_of[8], 71), 0),
        "values": draw_values(jax.random.fold_in(key_of[8], 71), 0),
        "w_in": normal_values(key_of[3], (EXPERTS, D, 2, FF), D ** -0.5, 0.09375, ((0, 64), (1, 4))),
        "w_out": normal_values(key_of[4], (EXPERTS, FF, D), FF ** -0.5, 0.21875, ((0, 64), (2, 4))),
        "routes": draw_routes(jax.random.fold_in(key_of[8], 71), 0),
        "route_weights": jnp.clip(0.05 + 0.39999999 * jax.random.uniform(key_of[6], (WINDOW_TOKENS, TOP), jnp.float32) ** block_levels(key_of[6], (WINDOW_TOKENS, TOP), ((0, 64),), -0.2, 0.2), 0.05, 0.45),
        "grad_out": normal_values(key_of[7], (WINDOW_TOKENS, D), 1.0, 6.0, ((0, 64), (1, 4))),
    }


norm_eps = 1e-05
hidden_logits = -1e+30

def settle(tensor):
    return lax.optimization_barrier(tensor.astype(jnp.bfloat16)).astype(jnp.float32)

def attend(queries, keys, values):
    grouping_width = QUERY_HEADS // KEY_VALUE_HEADS
    count_of_blocks = CACHE_POSITIONS // CACHE_PER_INDEX
    heads_of_queries = queries.astype(jnp.float32).reshape(WINDOW_TOKENS, KEY_VALUE_HEADS, grouping_width, HEAD_WIDTH)
    blocked_keys = keys.astype(jnp.float32).reshape(count_of_blocks, CACHE_PER_INDEX, KEY_VALUE_HEADS, HEAD_WIDTH)
    blocked_values = values.astype(jnp.float32).reshape(count_of_blocks, CACHE_PER_INDEX, KEY_VALUE_HEADS, HEAD_WIDTH)
    query_pos = CACHE_POSITIONS - WINDOW_TOKENS + jnp.arange(WINDOW_TOKENS, dtype=jnp.int32)

    def one_block(running, element):
        top_now, total_now, sums_now = running
        key_block, value_block, block_index = element
        key_pos = block_index * CACHE_PER_INDEX + jnp.arange(CACHE_PER_INDEX, dtype=jnp.int32)
        visible = (key_pos[None, :] <= query_pos[:, None])[:, None, None, :]
        scores = jnp.einsum('tgid,jgd->tgij', heads_of_queries, key_block) * HEAD_WIDTH ** (-0.5)
        scores = jnp.where(visible, scores, hidden_logits)
        block_top = settle(lax.optimization_barrier(jnp.max(scores, axis=-1)))
        weights = jnp.where(visible, jnp.exp(scores - block_top[..., None]), 0.0)
        block_total = settle(lax.optimization_barrier(jnp.sum(weights, axis=-1)))
        block_sum = settle(jnp.einsum('tgij,jgd->tgid', settle(weights), value_block))
        new_top = jnp.maximum(top_now, block_top)
        old_factor = jnp.exp(top_now - new_top)
        new_factor = jnp.exp(block_top - new_top)
        total_next = total_now * old_factor + block_total * new_factor
        sums_next = sums_now * old_factor[..., None] + block_sum * new_factor[..., None]
        return ((new_top, total_next, sums_next), None)
    beginning = (jnp.full((WINDOW_TOKENS, KEY_VALUE_HEADS, grouping_width), hidden_logits, jnp.float32), jnp.zeros((WINDOW_TOKENS, KEY_VALUE_HEADS, grouping_width), jnp.float32), jnp.zeros((WINDOW_TOKENS, KEY_VALUE_HEADS, grouping_width, HEAD_WIDTH), jnp.float32))
    running, ignored = lax.scan(one_block, beginning, (blocked_keys, blocked_values, jnp.arange(count_of_blocks, dtype=jnp.int32)))
    return (running[2] / running[1][..., None]).reshape(WINDOW_TOKENS, QUERY_HEADS * HEAD_WIDTH).astype(jnp.bfloat16)

def expert_pass(element):
    row_block, grad_block, w_first, w_second = element
    row_float = row_block.astype(jnp.float32)
    squares = lax.optimization_barrier(jnp.sum(row_float * row_float, axis=1))
    norm_scale = lax.rsqrt(squares / D + norm_eps)[:, None]
    raw_sums = jnp.dot(row_block, w_first.reshape(D, 2 * FF), preferred_element_type=jnp.float32).reshape(-1, 2, FF)
    gate_value = raw_sums[:, 0] * norm_scale
    up_value = raw_sums[:, 1] * norm_scale
    gate_sigmoid = jax.nn.sigmoid(gate_value)
    gate_silu = gate_value * gate_sigmoid
    hidden_act = (gate_silu * up_value).astype(jnp.bfloat16)
    out_rows = jnp.dot(hidden_act, w_second, preferred_element_type=jnp.float32).astype(jnp.bfloat16)
    back_sums = jnp.dot(grad_block, jnp.transpose(w_second), preferred_element_type=jnp.float32)
    grad_gate = back_sums * up_value * gate_sigmoid * (1.0 + gate_value * (1.0 - gate_sigmoid))
    grad_up = back_sums * gate_silu
    grad_hidden = jnp.stack([grad_gate, grad_up], axis=1).astype(jnp.bfloat16)
    grad_normed = jnp.dot(grad_hidden.reshape(-1, 2 * FF), jnp.transpose(w_first.reshape(D, 2 * FF)), preferred_element_type=jnp.float32)
    inner_sum = lax.optimization_barrier(jnp.sum(grad_hidden.astype(jnp.float32) * jnp.stack([gate_value, up_value], axis=1), axis=(1, 2)))
    grad_rows = norm_scale * grad_normed - row_float * (norm_scale * norm_scale / D) * inner_sum[:, None]
    return (out_rows, grad_rows.astype(jnp.bfloat16))

def reference(queries, keys, values, w_in, w_out, routes, route_weights, grad_out):
    attended = attend(queries, keys, values)
    shard_count = WINDOW_TOKENS // TOK_DEV
    shard_routes = routes.reshape(shard_count, TOK_DEV * TOP)
    expert_hits = (shard_routes[:, :, None] == jnp.arange(EXPERTS, dtype=jnp.int32)[None, None, :]).astype(jnp.int32)
    earlier = jnp.cumsum(expert_hits, axis=1) - expert_hits
    slot_index = lax.optimization_barrier(jnp.sum(earlier * expert_hits, axis=2)).astype(jnp.int32)
    row_of = (jnp.arange(shard_count, dtype=jnp.int32)[:, None] * CAP + slot_index).reshape(-1).astype(jnp.int32)
    expert_of = shard_routes.reshape(-1).astype(jnp.int32)
    token_of = jnp.repeat(jnp.arange(WINDOW_TOKENS, dtype=jnp.int32), TOP)
    slot_rows = shard_count * CAP
    row_table = jnp.zeros((EXPERTS, slot_rows, D), jnp.bfloat16).at[expert_of, row_of].set(attended[token_of])
    grad_table = jnp.zeros((EXPERTS, slot_rows, D), jnp.bfloat16).at[expert_of, row_of].set(grad_out[token_of])
    out_table, grad_rows = lax.map(expert_pass, (row_table, grad_table, w_in, w_out))
    picked_out = out_table[expert_of, row_of].astype(jnp.float32).reshape(WINDOW_TOKENS, TOP, D)
    picked_grad = grad_rows[expert_of, row_of].astype(jnp.float32).reshape(WINDOW_TOKENS, TOP, D)
    output = (attended.astype(jnp.float32) + lax.optimization_barrier(jnp.sum(route_weights[:, :, None] * picked_out, axis=1))).astype(jnp.bfloat16)
    grad_attended = (grad_out.astype(jnp.float32) + lax.optimization_barrier(jnp.sum(route_weights[:, :, None] * picked_grad, axis=1))).astype(jnp.bfloat16)
    return (output, grad_attended)
```

```python
import functools

import jax
import jax.numpy as jnp
import numpy as np
from jax import lax
from jax.experimental import pallas as pl
from jax.experimental.pallas import tpu as pltpu
from jax.sharding import PartitionSpec as P

D = 4096
HEAD_WIDTH = 128
TOP = 6
norm_eps = 1e-05
hidden_logits = -1e30

ROWS = 128
HEADS = 8
GROUPS = 2
WIDTH = 1024
FF = 768
EXPERTS = 64
CAP = 14
PIECES = 4
PIECE = WIDTH // PIECES
BUNCH = 8
COMPACT = BUNCH * CAP
SPREAD = BUNCH * CAP * PIECES
BUNCHES = EXPERTS // BUNCH
PLACES = EXPERTS * CAP
F32 = jnp.float32
BF16 = jnp.bfloat16
MIB = 1 << 20


def params(mib):
    return pltpu.CompilerParams(vmem_limit_bytes=mib * MIB)


def spread_matrix():
    spread = np.arange(SPREAD)
    compact = np.arange(COMPACT)
    source = spread // (CAP * PIECES) * CAP + spread % CAP
    piece = spread % (CAP * PIECES) // CAP
    same = source[:, None] == compact[None, :]
    return np.stack([same & (piece[:, None] == j) for j in range(PIECES)]).astype(np.float32)


def dot(a, b):
    return lax.dot_general(a, b, (((1,), (0,)), ((), ())), preferred_element_type=F32)


def dot_t(a, b):
    return lax.dot_general(a, b, (((1,), (1,)), ((), ())), preferred_element_type=F32)


CHUNK = 8


def attention_kernel(place_ref, q_ref, kv_ref, o_ref, q_s, m_s, l_s, acc_s):
    step = pl.program_id(0)
    place = place_ref[0]
    per_group = HEADS // GROUPS
    rows = per_group * ROWS
    keys = CHUNK * ROWS
    factor = HEAD_WIDTH**-0.5 * 1.4426950408889634

    @pl.when(step == 0)
    def _():
        for i in range(HEADS):
            g, a = divmod(i, per_group)
            q_s[g, a * ROWS : (a + 1) * ROWS, :] = q_ref[:, i * HEAD_WIDTH : (i + 1) * HEAD_WIDTH]
        m_s[...] = jnp.full(m_s.shape, hidden_logits, F32)
        l_s[...] = jnp.zeros(l_s.shape, F32)
        acc_s[...] = jnp.zeros(acc_s.shape, F32)

    def update(masked):
        for g in range(GROUPS):
            k = kv_ref[:, g * HEAD_WIDTH : (g + 1) * HEAD_WIDTH]
            v = kv_ref[:, (GROUPS + g) * HEAD_WIDTH : (GROUPS + g + 1) * HEAD_WIDTH]
            s = dot_t(q_s[g], k)
            if masked:
                row = lax.broadcasted_iota(jnp.int32, (rows, keys), 0) & (ROWS - 1)
                col = lax.broadcasted_iota(jnp.int32, (rows, keys), 1) + (step * CHUNK - place) * ROWS
                s = jnp.where(col <= row, s, hidden_logits)
            best = s[:, :ROWS]
            for b in range(1, CHUNK):
                best = jnp.maximum(best, s[:, b * ROWS : (b + 1) * ROWS])
            m_old = m_s[g]
            m_new = jnp.maximum(m_old, jnp.max(best, axis=1, keepdims=True))
            decay = jnp.exp2((m_old - m_new) * factor)
            m_s[g] = m_new
            m_col = m_new[:, :1] * factor
            p = jnp.exp2(s * factor - m_col)
            total = p[:, :ROWS]
            for b in range(1, CHUNK):
                total = total + p[:, b * ROWS : (b + 1) * ROWS]
            l_s[g] = l_s[g] * decay + total
            acc_s[g] = acc_s[g] * decay + dot(p.astype(BF16), v)

    @pl.when((step + 1) * CHUNK <= place)
    def _():
        update(False)

    @pl.when(((step + 1) * CHUNK > place) & (step * CHUNK <= place))
    def _():
        update(True)

    @pl.when(step == pl.num_programs(0) - 1)
    def _():
        for i in range(HEADS):
            g, a = divmod(i, per_group)
            at = slice(a * ROWS, (a + 1) * ROWS)
            total = jnp.sum(l_s[g, at, :], axis=1, keepdims=True)
            o_ref[:, i * HEAD_WIDTH : (i + 1) * HEAD_WIDTH] = (acc_s[g, at, :] / total).astype(BF16)


def attention(place, queries, kv):
    steps = kv.shape[0] // (CHUNK * ROWS)
    rows = HEADS // GROUPS * ROWS
    keys = CHUNK * ROWS
    return pl.pallas_call(
        attention_kernel,
        grid_spec=pltpu.PrefetchScalarGridSpec(
            num_scalar_prefetch=1,
            grid=(steps,),
            in_specs=[
                pl.BlockSpec((ROWS, WIDTH), lambda i, s: (0, 0)),
                pl.BlockSpec((keys, kv.shape[1]), lambda i, s: (jnp.minimum(i, s[0] // CHUNK), 0)),
            ],
            out_specs=pl.BlockSpec((ROWS, WIDTH), lambda i, s: (0, 0)),
            scratch_shapes=[
                pltpu.VMEM((GROUPS, rows, HEAD_WIDTH), BF16),
                pltpu.VMEM((GROUPS, rows, HEAD_WIDTH), F32),
                pltpu.VMEM((GROUPS, rows, HEAD_WIDTH), F32),
                pltpu.VMEM((GROUPS, rows, HEAD_WIDTH), F32),
            ],
        ),
        out_shape=jax.ShapeDtypeStruct((ROWS, WIDTH), BF16),
        compiler_params=params(40),
        name="attention",
    )(place, queries, kv)


def pieces_of(values):
    return [values[:, j * PIECE : (j + 1) * PIECE] for j in range(PIECES)]


def send_kernel(picker_ref, rows_ref, spread_ref, o_ref):
    for b in range(BUNCHES):
        picked = dot(picker_ref[b * COMPACT : (b + 1) * COMPACT, :], rows_ref[...]).astype(BF16)
        out = sum(dot(spread_ref[j], part) for j, part in enumerate(pieces_of(picked)))
        o_ref[b * SPREAD : (b + 1) * SPREAD, :] = out.astype(BF16)


def send_rows(picker, rows, spread):
    return pl.pallas_call(
        send_kernel,
        out_shape=jax.ShapeDtypeStruct((PLACES * PIECES, PIECE), BF16),
        compiler_params=params(32),
        name="send_rows",
    )(picker, rows, spread)


def gather_compact(source_ref, gather_ref, target_ref):
    for b in range(BUNCHES):
        part = source_ref[b * SPREAD : (b + 1) * SPREAD, :]
        for j in range(PIECES):
            target_ref[b * COMPACT : (b + 1) * COMPACT, j * PIECE : (j + 1) * PIECE] = dot(
                gather_ref[j], part
            ).astype(BF16)


TILE = 256


def first_kernel(by_rows, x_ref, gather_ref, w_ref, o_ref, compact_ref):
    @pl.when(pl.program_id(0) == 0)
    def _():
        gather_compact(x_ref, gather_ref, compact_ref)

    product = dot_t if by_rows else dot
    o_ref[...] = product(compact_ref[...], w_ref[...]).astype(BF16)


def first_product(x, gather, w, by_rows):
    if by_rows:
        outs = w.shape[0]
        w_spec = pl.BlockSpec((TILE, WIDTH), lambda i: (i, 0))
    else:
        outs = w.shape[1]
        w_spec = pl.BlockSpec((WIDTH, TILE), lambda i: (0, i))
    return pl.pallas_call(
        functools.partial(first_kernel, by_rows),
        grid=(outs // TILE,),
        in_specs=[
            pl.BlockSpec(x.shape, lambda i: (0, 0)),
            pl.BlockSpec(gather.shape, lambda i: (0, 0, 0)),
            w_spec,
        ],
        out_specs=[
            pl.BlockSpec((PLACES, TILE), lambda i: (0, i)),
            pl.BlockSpec((PLACES, WIDTH), lambda i: (0, 0)),
        ],
        out_shape=[
            jax.ShapeDtypeStruct((PLACES, outs), BF16),
            jax.ShapeDtypeStruct((PLACES, WIDTH), BF16),
        ],
        compiler_params=params(40),
        name="first_product",
    )(x, gather, w)


def second_kernel(by_rows, corrected, *refs):
    if corrected:
        h_ref, w_ref, spread_ref, row_ref, weight_ref, o_ref, y_s = refs
    else:
        h_ref, w_ref, spread_ref, o_ref, y_s = refs
    step = pl.program_id(0)
    product = dot_t if by_rows else dot
    y = product(h_ref[...], w_ref[...])
    if corrected:
        y = y - row_ref[...].astype(F32) * weight_ref[...]
    y_s[step] = y.astype(BF16)

    @pl.when(step == PIECES - 1)
    def _():
        for b in range(BUNCHES):
            out = sum(
                dot(spread_ref[j], y_s[j, b * COMPACT : (b + 1) * COMPACT, :]) for j in range(PIECES)
            )
            o_ref[b * SPREAD : (b + 1) * SPREAD, :] = out.astype(BF16)


def second_product(h, w, spread, by_rows, rows=None, weight=None):
    depth = h.shape[1]
    w_spec = (
        pl.BlockSpec((PIECE, depth), lambda i: (i, 0))
        if by_rows
        else pl.BlockSpec((depth, PIECE), lambda i: (0, i))
    )
    in_specs = [
        pl.BlockSpec(h.shape, lambda i: (0, 0)),
        w_spec,
        pl.BlockSpec(spread.shape, lambda i: (0, 0, 0)),
    ]
    args = [h, w, spread]
    if rows is not None:
        in_specs += [
            pl.BlockSpec((PLACES, PIECE), lambda i: (0, i)),
            pl.BlockSpec((PLACES, 1), lambda i: (0, 0)),
        ]
        args += [rows, weight]
    return pl.pallas_call(
        functools.partial(second_kernel, by_rows, rows is not None),
        grid=(PIECES,),
        in_specs=in_specs,
        out_specs=pl.BlockSpec((PLACES * PIECES, PIECE), lambda i: (0, 0)),
        out_shape=jax.ShapeDtypeStruct((PLACES * PIECES, PIECE), BF16),
        scratch_shapes=[pltpu.VMEM((PIECES, PLACES, PIECE), BF16)],
        compiler_params=params(40),
        name="second_product",
    )(*args)


def combine_kernel(came_ref, gather_ref, weight_ref, base_ref, o_ref, compact_s):
    gather_compact(came_ref, gather_ref, compact_s)
    both = dot(weight_ref[...], compact_s[...])
    o_ref[...] = (base_ref[...].astype(F32) + (both[:ROWS] + both[ROWS:])).astype(BF16)


def combine(came, gather, weight, base):
    return pl.pallas_call(
        combine_kernel,
        out_shape=jax.ShapeDtypeStruct((ROWS, WIDTH), BF16),
        scratch_shapes=[pltpu.VMEM((PLACES, WIDTH), BF16)],
        compiler_params=params(32),
        name="combine",
    )(came, gather, weight, base)


def exchange(x):
    y = lax.all_to_all(
        x.reshape(EXPERTS, CAP * PIECES, PIECE), "exp", split_axis=0, concat_axis=0, tiled=True
    )
    return y.reshape(PLACES * PIECES, PIECE)


def head_sum(x):
    count = lax.axis_size("head")
    total = x
    for d in range(1, count):
        total = total + lax.ppermute(x, "head", [(i, (i + d) % count) for i in range(count)])
    return total


def per_device(queries, keys, values, w_in, w_out, routes, route_weights, grad_out):
    place = lax.axis_index("exp").astype(jnp.int32)
    head = lax.axis_index("head")
    w_first = w_in[0].reshape(WIDTH, 2 * FF)
    w_second = w_out[0]
    matrix = spread_matrix()
    spread = jnp.asarray(matrix, BF16)
    gather = jnp.asarray(matrix.transpose(0, 2, 1), BF16)

    kv = lax.all_gather(jnp.concatenate([keys, values], axis=1), "exp", axis=0, tiled=True)

    hits = routes[:, :, None] == jnp.arange(EXPERTS, dtype=jnp.int32)
    hit = jnp.any(hits, axis=1)
    earlier = jnp.asarray(np.tril(np.ones((ROWS, ROWS), np.float32), -1), BF16)
    rank = dot(earlier, hit.astype(BF16))
    rank = jnp.where(hit, rank, -1.0)
    token_weight = jnp.sum(jnp.where(hits, route_weights[:, :, None], 0.0), axis=1)
    slots = jnp.arange(CAP, dtype=jnp.int32).astype(F32)
    picker = (rank.T[:, None, :] == slots[None, :, None]).astype(BF16).reshape(PLACES, ROWS)
    weight = jnp.where(rank[:, :, None] == slots, token_weight[:, :, None], 0.0).reshape(ROWS, PLACES)
    weight_high = weight.astype(BF16)
    weight_low = (weight - weight_high.astype(F32)).astype(BF16)
    weight_both = jnp.concatenate([weight_high, weight_low], axis=0)

    grads_in = exchange(send_rows(picker, grad_out, spread))
    back, _ = first_product(grads_in, gather, w_second, True)
    back = lax.psum_scatter(back, "head", scatter_dimension=0, tiled=True).astype(F32)

    attended = attention(place[None], queries, kv)

    rows_in = exchange(send_rows(picker, attended, spread))
    raw, rows = first_product(rows_in, gather, w_first, False)
    raw = lax.psum_scatter(raw, "head", scatter_dimension=0, tiled=True).astype(F32)
    rows_float = rows.astype(F32)
    squares = head_sum(jnp.sum(rows_float * rows_float, axis=1))
    scale_all = lax.rsqrt(squares / D + norm_eps)
    quarter = PLACES // lax.axis_size("head")
    scale = lax.dynamic_slice_in_dim(scale_all, head * quarter, quarter)[:, None]
    gate = raw[:, :FF] * scale
    up = raw[:, FF:] * scale
    sigmoid = jax.nn.sigmoid(gate)
    silu = gate * sigmoid
    act = (silu * up).astype(BF16)
    grad_gate = (back * up * sigmoid * (1.0 + gate * (1.0 - sigmoid)) * scale).astype(BF16)
    grad_up = (back * silu * scale).astype(BF16)
    inner = jnp.sum(grad_gate.astype(F32) * gate + grad_up.astype(F32) * up, axis=1)
    correction = inner * scale[:, 0] / D
    act = lax.all_gather(act, "head", axis=0, tiled=True)
    grad_hidden = lax.all_gather(
        jnp.concatenate([grad_gate, grad_up], axis=1), "head", axis=0, tiled=True
    )
    correction = lax.all_gather(correction, "head", axis=0, tiled=True)[:, None]

    came_out = exchange(second_product(act, w_second, spread, False))
    came_grad = exchange(
        second_product(grad_hidden, w_first, spread, True, rows, correction)
    )
    output = combine(came_out, gather, weight_both, attended)
    grad_attended = combine(came_grad, gather, weight_both, grad_out)
    return (output, grad_attended)


def solution(mesh):
    in_specs = (
        P("exp", "head"),
        P("exp", "head"),
        P("exp", "head"),
        P("exp", "head", None, None),
        P("exp", None, "head"),
        P("exp", None),
        P("exp", None),
        P("exp", "head"),
    )
    out_specs = (P("exp", "head"), P("exp", "head"))
    return jax.shard_map(
        per_device, mesh=mesh, in_specs=in_specs, out_specs=out_specs, check_vma=False
    )
```

```python
import functools

import jax
import jax.numpy as jnp
import numpy as np
from jax import lax
from jax.experimental import pallas as pl
from jax.experimental.pallas import tpu as pltpu
from jax.sharding import PartitionSpec as P

D = 4096
HEAD_WIDTH = 128
TOP = 6
norm_eps = 1e-05
hidden_logits = -1e30

ROWS = 128
HEADS = 8
GROUPS = 2
WIDTH = 1024
FF = 768
EXPERTS = 64
HEAD_COUNT = 4
CAP = 14
PIECES = 4
PIECE = WIDTH // PIECES
BUNCH = 8
COMPACT = BUNCH * CAP
SPREAD = BUNCH * CAP * PIECES
BUNCHES = EXPERTS // BUNCH
PLACES = EXPERTS * CAP
F32 = jnp.float32
BF16 = jnp.bfloat16
MIB = 1 << 20


def params(mib):
    return pltpu.CompilerParams(vmem_limit_bytes=mib * MIB)


def spread_matrix():
    spread = np.arange(SPREAD)
    compact = np.arange(COMPACT)
    source = spread // (CAP * PIECES) * CAP + spread % CAP
    piece = spread % (CAP * PIECES) // CAP
    same = source[:, None] == compact[None, :]
    return np.stack([same & (piece[:, None] == j) for j in range(PIECES)]).astype(np.float32)


def dot(a, b):
    return lax.dot_general(a, b, (((1,), (0,)), ((), ())), preferred_element_type=F32)


def dot_t(a, b):
    return lax.dot_general(a, b, (((1,), (1,)), ((), ())), preferred_element_type=F32)


def attention_kernel(sizes, diagonal, first, last, *refs):
    refs = list(refs)
    bias_ref, q_ref = refs[:2]
    pieces = refs[2 : 2 + len(sizes)]
    rest = refs[2 + len(sizes) :]
    if not first:
        olds, rest = rest[:3], rest[3:]
    if last:
        o_ref, rest = rest[0], rest[1:]
    m_s, l_s, acc_s, q_s = rest
    per_group = HEADS // GROUPS
    rows = per_group * ROWS
    factor = HEAD_WIDTH**-0.5 * 1.4426950408889634
    for i in range(HEADS):
        g, a = divmod(i, per_group)
        q_s[g, a * ROWS : (a + 1) * ROWS, :] = q_ref[:, i * HEAD_WIDTH : (i + 1) * HEAD_WIDTH]
    if first:
        m_s[...] = jnp.full(m_s.shape, hidden_logits, F32)
        l_s[...] = jnp.zeros(l_s.shape, F32)
        acc_s[...] = jnp.zeros(acc_s.shape, F32)
    else:
        m_s[...] = olds[0][...]
        l_s[...] = olds[1][...]
        acc_s[...] = olds[2][...]

    def update(index, kv_ref, start):
        count = sizes[index]
        for g in range(GROUPS):
            k = kv_ref[:, g * HEAD_WIDTH : (g + 1) * HEAD_WIDTH]
            v = kv_ref[:, (GROUPS + g) * HEAD_WIDTH : (GROUPS + g + 1) * HEAD_WIDTH]
            s = dot_t(q_s[g], k)
            parts = []
            for b in range(count):
                part = s[:, b * ROWS : (b + 1) * ROWS]
                if diagonal and index == 0 and b == 0:
                    row = lax.broadcasted_iota(jnp.int32, (rows, ROWS), 0) & (ROWS - 1)
                    col = lax.broadcasted_iota(jnp.int32, (rows, ROWS), 1)
                    part = jnp.where(col <= row, part, hidden_logits)
                else:
                    part = part + bias_ref[start + b]
                parts.append(part)
            best = functools.reduce(jnp.maximum, parts)
            m_old = m_s[g]
            m_new = jnp.maximum(m_old, jnp.max(best, axis=1, keepdims=True))
            decay = jnp.exp2((m_old - m_new) * factor)
            m_s[g] = m_new
            scaled = m_new * factor
            weights = [jnp.exp2(part * factor - scaled) for part in parts]
            l_s[g] = l_s[g] * decay + functools.reduce(jnp.add, weights)
            p = jnp.concatenate([w.astype(BF16) for w in weights], axis=1)
            acc_s[g] = acc_s[g] * decay + dot(p, v)

    start = 0
    for index, piece in enumerate(pieces):
        if diagonal and index == 0:
            update(index, piece, start)
        else:
            seen = bias_ref[start]
            for b in range(1, sizes[index]):
                seen = jnp.maximum(seen, bias_ref[start + b])

            @pl.when(seen > -1.0)
            def _(index=index, piece=piece, start=start):
                update(index, piece, start)

        start += sizes[index]

    if last:
        for i in range(HEADS):
            g, a = divmod(i, per_group)
            at = slice(a * ROWS, (a + 1) * ROWS)
            total = jnp.sum(l_s[g, at, :], axis=1, keepdims=True)
            o_ref[:, i * HEAD_WIDTH : (i + 1) * HEAD_WIDTH] = (acc_s[g, at, :] / total).astype(BF16)


def attend(place, queries, pieces, ids, state=None, last=False):
    sizes = tuple(piece.shape[0] // ROWS for piece in pieces)
    flat = jnp.stack([i for part in ids for i in part])
    bias = jnp.where(flat < place, 0.0, hidden_logits).astype(F32)
    shape = (GROUPS, HEADS // GROUPS * ROWS, HEAD_WIDTH)
    part = jax.ShapeDtypeStruct(shape, F32)
    state = state or ()
    blocks = sum(sizes)
    scratch = [pltpu.VMEM(shape, F32)] * 3 if last else []
    return pl.pallas_call(
        functools.partial(attention_kernel, sizes, not state, not state, last),
        in_specs=[pl.BlockSpec(memory_space=pltpu.SMEM)]
        + [pl.BlockSpec(memory_space=pltpu.VMEM)] * (1 + len(pieces) + len(state)),
        out_shape=jax.ShapeDtypeStruct((ROWS, WIDTH), BF16) if last else [part] * 3,
        scratch_shapes=scratch + [pltpu.VMEM(shape, BF16)],
        compiler_params=params(40),
        cost_estimate=pl.CostEstimate(
            flops=blocks * 2**27, bytes_accessed=blocks * 2**17, transcendentals=blocks * 2**17
        ),
        name="attention",
    )(bias, queries, *pieces, *state)


def shifted(z_count, x_count, dz=0, dx=0, swap=False):
    pairs = []
    for z in range(z_count):
        for x in range(x_count):
            for c in range(2):
                s = 2 * c - 1
                source = ((z + s * dz) % z_count, (x + s * dx) % x_count, 1 - c if swap else c)
                pairs.append((place_of(z_count, x_count, *source), place_of(z_count, x_count, z, x, c)))
    return pairs


def place_of(z_count, x_count, z, x, c):
    return (z % z_count * x_count + x % x_count) * 2 + c


def attention(place, queries, own):
    zs, xs = 8, 4
    along_z = lambda v: lax.ppermute(v, "exp", shifted(zs, xs, dz=1))
    along_x = lambda v: lax.ppermute(v, "exp", shifted(zs, xs, dx=1))
    swap = lambda v: lax.ppermute(v, "exp", shifted(zs, xs, swap=True))

    other = swap(own)
    pair = jnp.concatenate([own, other])
    r1 = along_z(pair)
    near = jnp.concatenate([own, r1, other, swap(r1)])
    near, r1 = lax.optimization_barrier((near, r1))
    near_x = along_x(near)
    r2 = along_z(r1)
    r3 = along_z(r2)
    lead, near_x = lax.optimization_barrier((r3[:ROWS], near_x))
    near_x2 = along_x(near_x[: near.shape[0] // 2])
    r4 = along_z(lead)
    half = jnp.concatenate([r2, r3, r4])
    far = jnp.concatenate([half, swap(half)])
    far, near_x = lax.optimization_barrier((far, near_x))
    far_x = along_x(far)

    z, x, c = place // (xs * 2), place // 2 % xs, place % 2

    def at(z, x, c):
        return (z % zs * xs + x % xs) * 2 + c

    def near_half(z, x, c):
        s = 2 * c - 1
        return [at(z, x, c), at(z + s, x, c), at(z + s, x, 1 - c)]

    def near_ids(z, x, c):
        s = 2 * c - 1
        return near_half(z, x, c) + [at(z, x, 1 - c), at(z - s, x, 1 - c), at(z - s, x, c)]

    def half_ids(z, x, c):
        s = 2 * c - 1
        return [
            at(z + 2 * s, x, c),
            at(z + 2 * s, x, 1 - c),
            at(z + 3 * s, x, c),
            at(z + 3 * s, x, 1 - c),
            at(z + 4 * s, x, c),
        ]

    def far_ids(z, x, c):
        return half_ids(z, x, c) + half_ids(z, x, 1 - c)

    s = 2 * c - 1
    state = attend(
        place,
        queries,
        [near, near_x, swap(near_x), near_x2, swap(near_x2)],
        [
            near_ids(z, x, c),
            near_ids(z, x + s, c),
            near_ids(z, x - s, 1 - c),
            near_half(z, x + 2 * s, c),
            near_half(z, x - 2 * s, 1 - c),
        ],
    )
    far_lead, state = lax.optimization_barrier((far_x[: half.shape[0]], state))
    far_x2 = along_x(far_lead)
    state = attend(
        place,
        queries,
        [far, far_x, swap(far_x)],
        [far_ids(z, x, c), far_ids(z, x + s, c), far_ids(z, x - s, 1 - c)],
        state,
    )
    return attend(
        place,
        queries,
        [far_x2, swap(far_x2)],
        [half_ids(z, x + 2 * s, c), half_ids(z, x - 2 * s, 1 - c)],
        state,
        True,
    )


def pieces_of(values):
    return [values[:, j * PIECE : (j + 1) * PIECE] for j in range(PIECES)]


def send_kernel(picker_ref, rows_ref, spread_ref, o_ref):
    for b in range(BUNCHES):
        picked = dot(picker_ref[b * COMPACT : (b + 1) * COMPACT, :], rows_ref[...]).astype(BF16)
        out = sum(dot(spread_ref[j], part) for j, part in enumerate(pieces_of(picked)))
        o_ref[b * SPREAD : (b + 1) * SPREAD, :] = out.astype(BF16)


def send_rows(picker, rows, spread):
    return pl.pallas_call(
        send_kernel,
        out_shape=jax.ShapeDtypeStruct((PLACES * PIECES, PIECE), BF16),
        compiler_params=params(32),
        name="send_rows",
    )(picker, rows, spread)


def gather_compact(source_ref, gather_ref, target_ref):
    for b in range(BUNCHES):
        part = source_ref[b * SPREAD : (b + 1) * SPREAD, :]
        for j in range(PIECES):
            target_ref[b * COMPACT : (b + 1) * COMPACT, j * PIECE : (j + 1) * PIECE] = dot(
                gather_ref[j], part
            ).astype(BF16)


TILE = 256


def first_kernel(by_rows, x_ref, gather_ref, w_ref, o_ref, compact_ref):
    @pl.when(pl.program_id(0) == 0)
    def _():
        gather_compact(x_ref, gather_ref, compact_ref)

    product = dot_t if by_rows else dot
    o_ref[...] = product(compact_ref[...], w_ref[...]).astype(BF16)


def first_product(x, gather, w, by_rows):
    if by_rows:
        outs = w.shape[0]
        w_spec = pl.BlockSpec((TILE, WIDTH), lambda i: (i, 0))
    else:
        outs = w.shape[1]
        w_spec = pl.BlockSpec((WIDTH, TILE), lambda i: (0, i))
    return pl.pallas_call(
        functools.partial(first_kernel, by_rows),
        grid=(outs // TILE,),
        in_specs=[
            pl.BlockSpec(x.shape, lambda i: (0, 0)),
            pl.BlockSpec(gather.shape, lambda i: (0, 0, 0)),
            w_spec,
        ],
        out_specs=[
            pl.BlockSpec((PLACES, TILE), lambda i: (0, i)),
            pl.BlockSpec((PLACES, WIDTH), lambda i: (0, 0)),
        ],
        out_shape=[
            jax.ShapeDtypeStruct((PLACES, outs), BF16),
            jax.ShapeDtypeStruct((PLACES, WIDTH), BF16),
        ],
        compiler_params=params(40),
        name="first_product",
    )(x, gather, w)


def second_kernel(by_rows, corrected, head_ref, *refs):
    pieces, refs = refs[:HEAD_COUNT], refs[HEAD_COUNT:]
    if corrected:
        w_ref, spread_ref, row_ref, o_ref, h_s, y_s, weight_s = refs
    else:
        w_ref, spread_ref, o_ref, h_s, y_s = refs
    step = pl.program_id(0)
    depth = h_s.shape[1]
    quarter = PLACES // HEAD_COUNT

    @pl.when(step == 0)
    def _():
        for d, piece in enumerate(pieces):
            at = lax.rem(head_ref[0] + d, HEAD_COUNT) * quarter
            at = pl.ds(pl.multiple_of(at, 16), quarter)
            h_s[at, :] = piece[:, :depth]
            if corrected:
                weight_s[at, :] = piece[:, depth : depth + 128].astype(F32)

    product = dot_t if by_rows else dot
    y = product(h_s[...], w_ref[...])
    if corrected:
        y = y - row_ref[...].astype(F32) * (weight_s[:, 0:1] + weight_s[:, 1:2])
    y_s[step] = y.astype(BF16)

    @pl.when(step == PIECES - 1)
    def _():
        for b in range(BUNCHES):
            out = sum(
                dot(spread_ref[j], y_s[j, b * COMPACT : (b + 1) * COMPACT, :]) for j in range(PIECES)
            )
            o_ref[b * SPREAD : (b + 1) * SPREAD, :] = out.astype(BF16)


def second_product(head, pieces, w, spread, by_rows, rows=None):
    depth = w.shape[1] if by_rows else w.shape[0]
    w_spec = (
        pl.BlockSpec((PIECE, depth), lambda i, s: (i, 0))
        if by_rows
        else pl.BlockSpec((depth, PIECE), lambda i, s: (0, i))
    )
    in_specs = [pl.BlockSpec(piece.shape, lambda i, s: (0, 0)) for piece in pieces] + [
        w_spec,
        pl.BlockSpec(spread.shape, lambda i, s: (0, 0, 0)),
    ]
    args = [*pieces, w, spread]
    scratch = [pltpu.VMEM((PLACES, depth), BF16), pltpu.VMEM((PIECES, PLACES, PIECE), BF16)]
    if rows is not None:
        in_specs += [pl.BlockSpec((PLACES, PIECE), lambda i, s: (0, i))]
        args += [rows]
        scratch += [pltpu.VMEM((PLACES, 128), F32)]
    return pl.pallas_call(
        functools.partial(second_kernel, by_rows, rows is not None),
        grid_spec=pltpu.PrefetchScalarGridSpec(
            num_scalar_prefetch=1,
            grid=(PIECES,),
            in_specs=in_specs,
            out_specs=pl.BlockSpec((PLACES * PIECES, PIECE), lambda i, s: (0, 0)),
            scratch_shapes=scratch,
        ),
        out_shape=jax.ShapeDtypeStruct((PLACES * PIECES, PIECE), BF16),
        compiler_params=params(40),
        name="second_product",
    )(head[None], *args)


def combine_kernel(came_ref, gather_ref, weight_ref, base_ref, o_ref, compact_s):
    gather_compact(came_ref, gather_ref, compact_s)
    both = dot(weight_ref[...], compact_s[...])
    o_ref[...] = (base_ref[...].astype(F32) + (both[:ROWS] + both[ROWS:])).astype(BF16)


def combine(came, gather, weight, base):
    return pl.pallas_call(
        combine_kernel,
        out_shape=jax.ShapeDtypeStruct((ROWS, WIDTH), BF16),
        scratch_shapes=[pltpu.VMEM((PLACES, WIDTH), BF16)],
        compiler_params=params(32),
        name="combine",
    )(came, gather, weight, base)


def exchange(x):
    y = lax.all_to_all(
        x.reshape(EXPERTS, CAP * PIECES, PIECE), "exp", split_axis=0, concat_axis=0, tiled=True
    )
    return y.reshape(PLACES * PIECES, PIECE)


def head_sum(x):
    count = lax.axis_size("head")
    total = x
    for d in range(1, count):
        total = total + lax.ppermute(x, "head", [(i, (i + d) % count) for i in range(count)])
    return total


def up(x):
    return lax.ppermute(x, "head", [(i, (i + 1) % HEAD_COUNT) for i in range(HEAD_COUNT)])


def down(x):
    return lax.ppermute(x, "head", [(i, (i - 1) % HEAD_COUNT) for i in range(HEAD_COUNT)])


def head_scatter(head, x):
    rows = x.shape[0] // HEAD_COUNT
    half = rows // 2

    def part(d, at, count):
        return lax.dynamic_slice_in_dim(x, (head + d) % HEAD_COUNT * rows + at, count)

    far_up = up(part(2, 0, half))
    far_down = down(part(2, half, half))
    from_low_late = up(part(1, half, half))
    from_high_early = down(part(-1, 0, half))
    from_low_early = up((part(1, 0, half).astype(F32) + far_up.astype(F32)).astype(BF16))
    from_high_late = down((part(-1, half, half).astype(F32) + far_down.astype(F32)).astype(BF16))
    early = from_low_early.astype(F32) + from_high_early.astype(F32)
    late = from_low_late.astype(F32) + from_high_late.astype(F32)
    return part(0, 0, rows).astype(F32) + jnp.concatenate([early, late])


def head_gather(x):
    half = x.shape[0] // 2
    low = up(x)
    high = down(x)
    opposite = jnp.concatenate([up(low[:half]), down(high[half:])])
    return [x, high, opposite, low]


def per_device(queries, keys, values, w_in, w_out, routes, route_weights, grad_out):
    place = lax.axis_index("exp").astype(jnp.int32)
    head = lax.axis_index("head").astype(jnp.int32)
    w_first = w_in[0].reshape(WIDTH, 2 * FF)
    w_second = w_out[0]
    matrix = spread_matrix()
    spread = jnp.asarray(matrix, BF16)
    gather = jnp.asarray(matrix.transpose(0, 2, 1), BF16)

    attended = attention(place, queries, jnp.concatenate([keys, values], axis=1))

    hits = routes[:, :, None] == jnp.arange(EXPERTS, dtype=jnp.int32)
    hit = jnp.any(hits, axis=1)
    earlier = jnp.asarray(np.tril(np.ones((ROWS, ROWS), np.float32), -1), BF16)
    rank = dot(earlier, hit.astype(BF16))
    rank = jnp.where(hit, rank, -1.0)
    token_weight = jnp.sum(jnp.where(hits, route_weights[:, :, None], 0.0), axis=1)
    slots = jnp.arange(CAP, dtype=jnp.int32).astype(F32)
    picker = (rank.T[:, None, :] == slots[None, :, None]).astype(BF16).reshape(PLACES, ROWS)
    weight = jnp.where(rank[:, :, None] == slots, token_weight[:, :, None], 0.0).reshape(ROWS, PLACES)
    weight_high = weight.astype(BF16)
    weight_low = (weight - weight_high.astype(F32)).astype(BF16)
    weight_both = jnp.concatenate([weight_high, weight_low], axis=0)

    rows_in = exchange(send_rows(picker, attended, spread))
    sent_grads, rows_in = lax.optimization_barrier((send_rows(picker, grad_out, spread), rows_in))
    grads_in = exchange(sent_grads)
    raw, rows = first_product(rows_in, gather, w_first, False)
    raw = head_scatter(head, raw)
    rows_float = rows.astype(F32)
    squares = head_sum(jnp.sum(rows_float * rows_float, axis=1))
    scale_all = lax.rsqrt(squares / D + norm_eps)
    quarter = PLACES // HEAD_COUNT
    scale = lax.dynamic_slice_in_dim(scale_all, head * quarter, quarter)[:, None]
    gate = raw[:, :FF] * scale
    lift = raw[:, FF:] * scale
    sigmoid = jax.nn.sigmoid(gate)
    silu = gate * sigmoid
    act = (silu * lift).astype(BF16)
    gathered = head_gather(act)
    grads_in, gathered[0] = lax.optimization_barrier((grads_in, act))
    came_out = exchange(second_product(head, gathered, w_second, spread, False))

    back, _ = first_product(grads_in, gather, w_second, True)
    back = head_scatter(head, back)
    grad_gate = (back * lift * sigmoid * (1.0 + gate * (1.0 - sigmoid)) * scale).astype(BF16)
    grad_up = (back * silu * scale).astype(BF16)
    inner = jnp.sum(
        grad_gate.astype(F32) * gate + grad_up.astype(F32) * lift, axis=1, keepdims=True
    )
    correction = inner * scale / D
    high = correction.astype(BF16)
    low = (correction - high.astype(F32)).astype(BF16)
    column = jnp.arange(128)[None, :]
    extra = jnp.where(column == 0, high, jnp.where(column == 1, low, jnp.zeros_like(low)))
    grad_hidden = head_gather(jnp.concatenate([grad_gate, grad_up, extra], axis=1))
    came_grad = exchange(second_product(head, grad_hidden, w_first, spread, True, rows))
    output = combine(came_out, gather, weight_both, attended)
    grad_attended = combine(came_grad, gather, weight_both, grad_out)
    return (output, grad_attended)


def solution(mesh):
    in_specs = (
        P("exp", "head"),
        P("exp", "head"),
        P("exp", "head"),
        P("exp", "head", None, None),
        P("exp", None, "head"),
        P("exp", None),
        P("exp", None),
        P("exp", "head"),
    )
    out_specs = (P("exp", "head"), P("exp", "head"))
    return jax.shard_map(
        per_device, mesh=mesh, in_specs=in_specs, out_specs=out_specs, check_vma=False
    )
```

```python
import functools

import jax
import jax.numpy as jnp
import numpy as np
from jax import lax
from jax.experimental import pallas as pl
from jax.experimental.pallas import tpu as pltpu
from jax.sharding import PartitionSpec as P

D = 4096
HEAD_WIDTH = 128
TOP = 6
norm_eps = 1e-05
hidden_logits = -1e30

ROWS = 128
HALF = ROWS // 2
HEADS = 8
GROUPS = 2
WIDTH = 1024
FF = 768
EXPERTS = 64
HEAD_COUNT = 4
CAP = 14
PIECES = 4
PIECE = WIDTH // PIECES
BUNCH = 8
COMPACT = BUNCH * CAP
SPREAD = BUNCH * CAP * PIECES
BUNCHES = EXPERTS // BUNCH
PLACES = EXPERTS * CAP
F32 = jnp.float32
BF16 = jnp.bfloat16
MIB = 1 << 20


def params(mib):
    return pltpu.CompilerParams(vmem_limit_bytes=mib * MIB)


def spread_matrix():
    spread = np.arange(SPREAD)
    compact = np.arange(COMPACT)
    source = spread // (CAP * PIECES) * CAP + spread % CAP
    piece = spread % (CAP * PIECES) // CAP
    same = source[:, None] == compact[None, :]
    return np.stack([same & (piece[:, None] == j) for j in range(PIECES)]).astype(np.float32)


def dot(a, b):
    return lax.dot_general(a, b, (((1,), (0,)), ((), ())), preferred_element_type=F32)


def dot_t(a, b):
    return lax.dot_general(a, b, (((1,), (1,)), ((), ())), preferred_element_type=F32)


def attention_kernel(sizes, diagonals, first, last, *refs):
    refs = list(refs)
    seen_ref, bias_ref, q_ref = refs[:3]
    refs = refs[1:]
    pieces = refs[2 : 2 + len(sizes)]
    rest = refs[2 + len(sizes) :]
    if not first:
        olds, rest = rest[:3], rest[3:]
    if last:
        o_ref, rest = rest[0], rest[1:]
    m_s, l_s, acc_s, q_s = rest
    per_group = HEADS // GROUPS
    rows = per_group * ROWS
    factor = HEAD_WIDTH**-0.5 * 1.4426950408889634
    for i in range(HEADS):
        g, a = divmod(i, per_group)
        q_s[g, a * ROWS : (a + 1) * ROWS, :] = q_ref[:, i * HEAD_WIDTH : (i + 1) * HEAD_WIDTH]
    if first:
        m_s[...] = jnp.full(m_s.shape, hidden_logits, F32)
        l_s[...] = jnp.zeros(l_s.shape, F32)
        acc_s[...] = jnp.zeros(acc_s.shape, F32)
    else:
        m_s[...] = olds[0][...]
        l_s[...] = olds[1][...]
        acc_s[...] = olds[2][...]

    def update(index, kv_ref, start):
        count = sizes[index]
        for g in range(GROUPS):
            k = kv_ref[:, g * HEAD_WIDTH : (g + 1) * HEAD_WIDTH]
            v = kv_ref[:, (GROUPS + g) * HEAD_WIDTH : (GROUPS + g + 1) * HEAD_WIDTH]
            s = dot_t(q_s[g], k)
            parts = []
            for b in range(count):
                part = s[:, b * ROWS : (b + 1) * ROWS]
                part = part + bias_ref[0:1, start + b * ROWS : start + (b + 1) * ROWS]
                if index in diagonals and b == 0:
                    row = lax.broadcasted_iota(jnp.int32, (rows, ROWS), 0) & (ROWS - 1)
                    col = lax.broadcasted_iota(jnp.int32, (rows, ROWS), 1)
                    after = (col < HALF) & (col + diagonals[index] > row)
                    part = jnp.where(after, hidden_logits, part)
                parts.append(part)
            best = functools.reduce(jnp.maximum, parts)
            m_old = m_s[g]
            m_new = jnp.maximum(m_old, jnp.max(best, axis=1, keepdims=True))
            decay = jnp.exp2((m_old - m_new) * factor)
            m_s[g] = m_new
            scaled = m_new * factor
            weights = [jnp.exp2(part * factor - scaled) for part in parts]
            l_s[g] = l_s[g] * decay + functools.reduce(jnp.add, weights)
            p = jnp.concatenate([w.astype(BF16) for w in weights], axis=1)
            acc_s[g] = acc_s[g] * decay + dot(p, v)

    start = 0
    for index, piece in enumerate(pieces):
        if index in diagonals:
            update(index, piece, start)
        else:

            @pl.when(seen_ref[index] > 0)
            def _(index=index, piece=piece, start=start):
                update(index, piece, start)

        start += sizes[index] * ROWS

    if last:
        for i in range(HEADS):
            g, a = divmod(i, per_group)
            at = slice(a * ROWS, (a + 1) * ROWS)
            total = jnp.sum(l_s[g, at, :], axis=1, keepdims=True)
            o_ref[:, i * HEAD_WIDTH : (i + 1) * HEAD_WIDTH] = (acc_s[g, at, :] / total).astype(BF16)


def attend(place, queries, pieces, ids, state=None, diagonals=(), last=False):
    sizes = tuple(piece.shape[0] // ROWS for piece in pieces)
    seen = jnp.stack([jnp.any(jnp.stack(part) < place) for part in ids]).astype(jnp.int32)
    flat = jnp.stack([i for part in ids for i in part])
    own = flat == place if diagonals else False
    bias = jnp.where((flat < place) | own, 0.0, hidden_logits).astype(F32)
    bias = jnp.broadcast_to(bias[:, None], (flat.shape[0], HALF)).reshape(1, -1)
    shape = (GROUPS, HEADS // GROUPS * ROWS, HEAD_WIDTH)
    part = jax.ShapeDtypeStruct(shape, F32)
    state = state or ()
    blocks = sum(sizes)
    scratch = [pltpu.VMEM(shape, F32)] * 3 if last else []
    return pl.pallas_call(
        functools.partial(attention_kernel, sizes, dict(diagonals), not state, last),
        in_specs=[pl.BlockSpec(memory_space=pltpu.SMEM)]
        + [pl.BlockSpec(memory_space=pltpu.VMEM)] * (2 + len(pieces) + len(state)),
        out_shape=jax.ShapeDtypeStruct((ROWS, WIDTH), BF16) if last else [part] * 3,
        scratch_shapes=scratch + [pltpu.VMEM(shape, BF16)],
        compiler_params=params(40),
        cost_estimate=pl.CostEstimate(
            flops=blocks * 2**27, bytes_accessed=blocks * 2**17, transcendentals=blocks * 2**17
        ),
        name="attention",
    )(seen, bias, queries, *pieces, *state)


def shifted(z_count, x_count, dz=0, dx=0, swap=False):
    pairs = []
    for z in range(z_count):
        for x in range(x_count):
            for c in range(2):
                s = 2 * c - 1
                source = ((z + s * dz) % z_count, (x + s * dx) % x_count, 1 - c if swap else c)
                pairs.append((place_of(z_count, x_count, *source), place_of(z_count, x_count, z, x, c)))
    return pairs


def place_of(z_count, x_count, z, x, c):
    return (z % z_count * x_count + x % x_count) * 2 + c


def attention(place, queries, own):
    zs, xs = 8, 4
    along_z = lambda v: lax.ppermute(v, "exp", shifted(zs, xs, dz=1))
    along_x = lambda v: lax.ppermute(v, "exp", shifted(zs, xs, dx=1))
    swap = lambda v: lax.ppermute(v, "exp", shifted(zs, xs, swap=True))
    tie = lax.optimization_barrier

    z, x, c = place // (xs * 2), place // 2 % xs, place % 2
    s = 2 * c - 1

    def at(z, x, c):
        return (z % zs * xs + x % xs) * 2 + c

    def low_half(z, x, c):
        s = 2 * c - 1
        ids = [at(z, x, c)]
        for d in (1, 2, 3):
            ids += [at(z + d * s, x, c), at(z + d * s, x, 1 - c)]
        return ids + [at(z + 4 * s, x, c)]

    def low_full(z, x, c):
        return low_half(z, x, c) + low_half(z, x, 1 - c)

    def high_half(z, x, c):
        s = 2 * c - 1
        return [at(z, x, c), at(z, x + s, c), at(z, x + s, 1 - c), at(z, x + 2 * s, c)]

    def high_full(z, x, c):
        return high_half(z, x, c) + high_half(z, x, 1 - c)

    other = swap(own)
    low1 = along_z(jnp.concatenate([own[:HALF], other[:HALF]]))
    high1 = along_x(jnp.concatenate([own[HALF:], other[HALF:]]))
    low2 = along_z(low1)
    high2 = along_x(high1[:HALF])
    low3 = along_z(low2)
    half_high = jnp.concatenate([own[HALF:], high1, high2])
    full_high = jnp.concatenate([half_high, swap(half_high)])
    low4 = along_z(low3[:HALF])
    z1 = along_z(full_high)
    half_low = jnp.concatenate([own[:HALF], low1, low2, low3, low4])
    full_low = jnp.concatenate([half_low, swap(half_low)])
    x1 = along_x(full_low)
    z2 = along_z(z1)
    state = attend(
        place,
        queries,
        [full_low, full_high, z1, swap(z1)],
        [low_full(z, x, c), high_full(z, x, c), high_full(z + s, x, c), high_full(z - s, x, 1 - c)],
        diagonals=((0, 0), (1, HALF)),
    )
    z2, top = tie((z2, state[0]))
    x1, total, sums = tie((x1, state[1], state[2]))
    z3 = along_z(z2)
    x2 = along_x(x1[: half_low.shape[0]])
    z4 = along_z(z3[: half_high.shape[0]])
    state = attend(
        place,
        queries,
        [z2, swap(z2), x1, swap(x1)],
        [
            high_full(z + 2 * s, x, c),
            high_full(z - 2 * s, x, 1 - c),
            low_full(z, x + s, c),
            low_full(z, x - s, 1 - c),
        ],
        (top, total, sums),
    )
    z4, top = tie((z4, state[0]))
    x2, total, sums = tie((x2, state[1], state[2]))
    return attend(
        place,
        queries,
        [z3, swap(z3), z4, swap(z4), x2, swap(x2)],
        [
            high_full(z + 3 * s, x, c),
            high_full(z - 3 * s, x, 1 - c),
            high_half(z + 4 * s, x, c),
            high_half(z - 4 * s, x, 1 - c),
            low_half(z, x + 2 * s, c),
            low_half(z, x - 2 * s, 1 - c),
        ],
        (top, total, sums),
        last=True,
    )


def pieces_of(values):
    return [values[:, j * PIECE : (j + 1) * PIECE] for j in range(PIECES)]


def send_kernel(picker_ref, rows_ref, spread_ref, o_ref):
    for b in range(BUNCHES):
        picked = dot(picker_ref[b * COMPACT : (b + 1) * COMPACT, :], rows_ref[...]).astype(BF16)
        out = sum(dot(spread_ref[j], part) for j, part in enumerate(pieces_of(picked)))
        o_ref[b * SPREAD : (b + 1) * SPREAD, :] = out.astype(BF16)


def send_rows(picker, rows, spread):
    return pl.pallas_call(
        send_kernel,
        out_shape=jax.ShapeDtypeStruct((PLACES * PIECES, PIECE), BF16),
        compiler_params=params(32),
        name="send_rows",
    )(picker, rows, spread)


def gather_compact(source_ref, gather_ref, target_ref):
    for b in range(BUNCHES):
        part = source_ref[b * SPREAD : (b + 1) * SPREAD, :]
        for j in range(PIECES):
            target_ref[b * COMPACT : (b + 1) * COMPACT, j * PIECE : (j + 1) * PIECE] = dot(
                gather_ref[j], part
            ).astype(BF16)


TILE = 256


def first_kernel(by_rows, x_ref, gather_ref, w_ref, o_ref, compact_ref):
    @pl.when(pl.program_id(0) == 0)
    def _():
        gather_compact(x_ref, gather_ref, compact_ref)

    product = dot_t if by_rows else dot
    o_ref[...] = product(compact_ref[...], w_ref[...]).astype(BF16)


def first_product(x, gather, w, by_rows):
    if by_rows:
        outs = w.shape[0]
        w_spec = pl.BlockSpec((TILE, WIDTH), lambda i: (i, 0))
    else:
        outs = w.shape[1]
        w_spec = pl.BlockSpec((WIDTH, TILE), lambda i: (0, i))
    return pl.pallas_call(
        functools.partial(first_kernel, by_rows),
        grid=(outs // TILE,),
        in_specs=[
            pl.BlockSpec(x.shape, lambda i: (0, 0)),
            pl.BlockSpec(gather.shape, lambda i: (0, 0, 0)),
            w_spec,
        ],
        out_specs=[
            pl.BlockSpec((PLACES, TILE), lambda i: (0, i)),
            pl.BlockSpec((PLACES, WIDTH), lambda i: (0, 0)),
        ],
        out_shape=[
            jax.ShapeDtypeStruct((PLACES, outs), BF16),
            jax.ShapeDtypeStruct((PLACES, WIDTH), BF16),
        ],
        compiler_params=params(40),
        name="first_product",
    )(x, gather, w)


def second_kernel(by_rows, corrected, head_ref, *refs):
    pieces, refs = refs[:HEAD_COUNT], refs[HEAD_COUNT:]
    if corrected:
        w_ref, spread_ref, row_ref, o_ref, h_s, y_s, weight_s = refs
    else:
        w_ref, spread_ref, o_ref, h_s, y_s = refs
    step = pl.program_id(0)
    depth = h_s.shape[1]
    quarter = PLACES // HEAD_COUNT

    @pl.when(step == 0)
    def _():
        for d, piece in enumerate(pieces):
            at = lax.rem(head_ref[0] + d, HEAD_COUNT) * quarter
            at = pl.ds(pl.multiple_of(at, 16), quarter)
            h_s[at, :] = piece[:, :depth]
            if corrected:
                weight_s[at, :] = piece[:, depth : depth + 128].astype(F32)

    product = dot_t if by_rows else dot
    y = product(h_s[...], w_ref[...])
    if corrected:
        y = y - row_ref[...].astype(F32) * (weight_s[:, 0:1] + weight_s[:, 1:2])
    y_s[step] = y.astype(BF16)

    @pl.when(step == PIECES - 1)
    def _():
        for b in range(BUNCHES):
            out = sum(
                dot(spread_ref[j], y_s[j, b * COMPACT : (b + 1) * COMPACT, :]) for j in range(PIECES)
            )
            o_ref[b * SPREAD : (b + 1) * SPREAD, :] = out.astype(BF16)


def second_product(head, pieces, w, spread, by_rows, rows=None):
    depth = w.shape[1] if by_rows else w.shape[0]
    w_spec = (
        pl.BlockSpec((PIECE, depth), lambda i, s: (i, 0))
        if by_rows
        else pl.BlockSpec((depth, PIECE), lambda i, s: (0, i))
    )
    in_specs = [pl.BlockSpec(piece.shape, lambda i, s: (0, 0)) for piece in pieces] + [
        w_spec,
        pl.BlockSpec(spread.shape, lambda i, s: (0, 0, 0)),
    ]
    args = [*pieces, w, spread]
    scratch = [pltpu.VMEM((PLACES, depth), BF16), pltpu.VMEM((PIECES, PLACES, PIECE), BF16)]
    if rows is not None:
        in_specs += [pl.BlockSpec((PLACES, PIECE), lambda i, s: (0, i))]
        args += [rows]
        scratch += [pltpu.VMEM((PLACES, 128), F32)]
    return pl.pallas_call(
        functools.partial(second_kernel, by_rows, rows is not None),
        grid_spec=pltpu.PrefetchScalarGridSpec(
            num_scalar_prefetch=1,
            grid=(PIECES,),
            in_specs=in_specs,
            out_specs=pl.BlockSpec((PLACES * PIECES, PIECE), lambda i, s: (0, 0)),
            scratch_shapes=scratch,
        ),
        out_shape=jax.ShapeDtypeStruct((PLACES * PIECES, PIECE), BF16),
        compiler_params=params(40),
        name="second_product",
    )(head[None], *args)


def combine_kernel(came_ref, gather_ref, weight_ref, base_ref, o_ref, compact_s):
    gather_compact(came_ref, gather_ref, compact_s)
    both = dot(weight_ref[...], compact_s[...])
    o_ref[...] = (base_ref[...].astype(F32) + (both[:ROWS] + both[ROWS:])).astype(BF16)


def combine(came, gather, weight, base):
    return pl.pallas_call(
        combine_kernel,
        out_shape=jax.ShapeDtypeStruct((ROWS, WIDTH), BF16),
        scratch_shapes=[pltpu.VMEM((PLACES, WIDTH), BF16)],
        compiler_params=params(32),
        name="combine",
    )(came, gather, weight, base)


def exchange(x):
    y = lax.all_to_all(
        x.reshape(EXPERTS, CAP * PIECES, PIECE), "exp", split_axis=0, concat_axis=0, tiled=True
    )
    return y.reshape(PLACES * PIECES, PIECE)


def head_sum(x):
    count = lax.axis_size("head")
    total = x
    for d in range(1, count):
        total = total + lax.ppermute(x, "head", [(i, (i + d) % count) for i in range(count)])
    return total


def up(x):
    return lax.ppermute(x, "head", [(i, (i + 1) % HEAD_COUNT) for i in range(HEAD_COUNT)])


def down(x):
    return lax.ppermute(x, "head", [(i, (i - 1) % HEAD_COUNT) for i in range(HEAD_COUNT)])


def head_scatter(head, x, after=None):
    rows = x.shape[0] // HEAD_COUNT
    half = rows // 2

    def part(d, at, count):
        return lax.dynamic_slice_in_dim(x, (head + d) % HEAD_COUNT * rows + at, count)

    low = up(jnp.concatenate([part(2, 0, half), part(1, half, half)]))
    high = down(jnp.concatenate([part(2, half, half), part(-1, 0, half)]))
    if after is not None:
        low, high, after = lax.optimization_barrier((low, high, after))
    low2 = up((part(1, 0, half).astype(F32) + low[:half].astype(F32)).astype(BF16))
    high2 = down((part(-1, half, half).astype(F32) + high[:half].astype(F32)).astype(BF16))
    early = low2.astype(F32) + high[half:].astype(F32)
    late = low[half:].astype(F32) + high2.astype(F32)
    return part(0, 0, rows).astype(F32) + jnp.concatenate([early, late]), after


def head_gather(x):
    half = x.shape[0] // 2
    low = up(x)
    high = down(x)
    opposite = jnp.concatenate([up(low[:half]), down(high[half:])])
    return [x, high, opposite, low]


def per_device(queries, keys, values, w_in, w_out, routes, route_weights, grad_out):
    place = lax.axis_index("exp").astype(jnp.int32)
    head = lax.axis_index("head").astype(jnp.int32)
    w_first = w_in[0].reshape(WIDTH, 2 * FF)
    w_second = w_out[0]
    matrix = spread_matrix()
    spread = jnp.asarray(matrix, BF16)
    gather = jnp.asarray(matrix.transpose(0, 2, 1), BF16)

    hits = routes[:, :, None] == jnp.arange(EXPERTS, dtype=jnp.int32)
    hit = jnp.any(hits, axis=1)
    earlier = jnp.asarray(np.tril(np.ones((ROWS, ROWS), np.float32), -1), BF16)
    rank = dot(earlier, hit.astype(BF16))
    rank = jnp.where(hit, rank, -1.0)
    token_weight = jnp.sum(jnp.where(hits, route_weights[:, :, None], 0.0), axis=1)
    slots = jnp.arange(CAP, dtype=jnp.int32).astype(F32)
    picker = (rank.T[:, None, :] == slots[None, :, None]).astype(BF16).reshape(PLACES, ROWS)
    weight = jnp.where(rank[:, :, None] == slots, token_weight[:, :, None], 0.0).reshape(ROWS, PLACES)
    weight_high = weight.astype(BF16)
    weight_low = (weight - weight_high.astype(F32)).astype(BF16)
    weight_both = jnp.concatenate([weight_high, weight_low], axis=0)

    sent_grads = send_rows(picker, grad_out, spread)
    queries, picker, weight_both, sent_grads = lax.optimization_barrier(
        (queries, picker, weight_both, sent_grads)
    )
    attended = attention(place, queries, jnp.concatenate([keys, values], axis=1))

    rows_in = exchange(send_rows(picker, attended, spread))
    sent_grads, rows_in = lax.optimization_barrier((sent_grads, rows_in))
    grads_in = exchange(sent_grads)
    raw, rows = first_product(rows_in, gather, w_first, False)
    raw, _ = head_scatter(head, raw)
    rows_float = rows.astype(F32)
    squares = head_sum(jnp.sum(rows_float * rows_float, axis=1))
    scale_all = lax.rsqrt(squares / D + norm_eps)
    quarter = PLACES // HEAD_COUNT
    scale = lax.dynamic_slice_in_dim(scale_all, head * quarter, quarter)[:, None]
    gate = raw[:, :FF] * scale
    lift = raw[:, FF:] * scale
    sigmoid = jax.nn.sigmoid(gate)
    silu = gate * sigmoid
    act = (silu * lift).astype(BF16)
    gathered = head_gather(act)
    grads_in, act = lax.optimization_barrier((grads_in, act))
    back, _ = first_product(grads_in, gather, w_second, True)
    back, gathered[0] = head_scatter(head, back, act)
    came_out = exchange(second_product(head, gathered, w_second, spread, False))
    grad_gate = (back * lift * sigmoid * (1.0 + gate * (1.0 - sigmoid)) * scale).astype(BF16)
    grad_up = (back * silu * scale).astype(BF16)
    inner = jnp.sum(
        grad_gate.astype(F32) * gate + grad_up.astype(F32) * lift, axis=1, keepdims=True
    )
    correction = inner * scale / D
    high = correction.astype(BF16)
    low = (correction - high.astype(F32)).astype(BF16)
    column = jnp.arange(128)[None, :]
    extra = jnp.where(column == 0, high, jnp.where(column == 1, low, jnp.zeros_like(low)))
    grad_hidden = head_gather(jnp.concatenate([grad_gate, grad_up, extra], axis=1))
    came_grad = exchange(second_product(head, grad_hidden, w_first, spread, True, rows))
    output = combine(came_out, gather, weight_both, attended)
    grad_attended = combine(came_grad, gather, weight_both, grad_out)
    return (output, grad_attended)


def solution(mesh):
    in_specs = (
        P("exp", "head"),
        P("exp", "head"),
        P("exp", "head"),
        P("exp", "head", None, None),
        P("exp", None, "head"),
        P("exp", None),
        P("exp", None),
        P("exp", "head"),
    )
    out_specs = (P("exp", "head"), P("exp", "head"))
    return jax.shard_map(
        per_device, mesh=mesh, in_specs=in_specs, out_specs=out_specs, check_vma=False
    )
```

```python
import functools

import jax
import jax.numpy as jnp
import numpy as np
from jax import lax
from jax.experimental import pallas as pl
from jax.experimental.pallas import tpu as pltpu
from jax.sharding import PartitionSpec as P

D = 4096
HEAD_WIDTH = 128
TOP = 6
norm_eps = 1e-05
hidden_logits = -1e30

ROWS = 128
HALF = ROWS // 2
HEADS = 8
GROUPS = 2
WIDTH = 1024
FF = 768
EXPERTS = 64
HEAD_COUNT = 4
CAP = 14
PIECES = 4
PIECE = WIDTH // PIECES
BUNCH = 8
COMPACT = BUNCH * CAP
SPREAD = BUNCH * CAP * PIECES
BUNCHES = EXPERTS // BUNCH
PLACES = EXPERTS * CAP
F32 = jnp.float32
BF16 = jnp.bfloat16
MIB = 1 << 20


def params(mib):
    return pltpu.CompilerParams(vmem_limit_bytes=mib * MIB)


def spread_matrix():
    spread = np.arange(SPREAD)
    compact = np.arange(COMPACT)
    source = spread // (CAP * PIECES) * CAP + spread % CAP
    piece = spread % (CAP * PIECES) // CAP
    same = source[:, None] == compact[None, :]
    return np.stack([same & (piece[:, None] == j) for j in range(PIECES)]).astype(np.float32)


def dot(a, b):
    return lax.dot_general(a, b, (((1,), (0,)), ((), ())), preferred_element_type=F32)


def dot_t(a, b):
    return lax.dot_general(a, b, (((1,), (1,)), ((), ())), preferred_element_type=F32)


def attention_kernel(sizes, diagonals, offset, first, last, *refs):
    refs = list(refs)
    bias_ref, q_ref = refs[:2]
    pieces = refs[2 : 2 + len(sizes)]
    rest = refs[2 + len(sizes) :]
    if not first:
        olds, rest = rest[:3], rest[3:]
    if last:
        o_ref, rest = rest[0], rest[1:]
    m_s, l_s, acc_s, q_s = rest
    per_group = HEADS // GROUPS
    rows = per_group * ROWS
    factor = HEAD_WIDTH**-0.5 * 1.4426950408889634
    for i in range(HEADS):
        g, a = divmod(i, per_group)
        q_s[g, a * ROWS : (a + 1) * ROWS, :] = q_ref[:, i * HEAD_WIDTH : (i + 1) * HEAD_WIDTH]
    if first:
        m_s[...] = jnp.full(m_s.shape, hidden_logits, F32)
        l_s[...] = jnp.zeros(l_s.shape, F32)
        acc_s[...] = jnp.zeros(acc_s.shape, F32)
    else:
        m_s[...] = olds[0][...]
        l_s[...] = olds[1][...]
        acc_s[...] = olds[2][...]

    def update(index, kv_ref, start):
        count = sizes[index]
        for g in range(GROUPS):
            k = kv_ref[:, g * HEAD_WIDTH : (g + 1) * HEAD_WIDTH]
            v = kv_ref[:, (GROUPS + g) * HEAD_WIDTH : (GROUPS + g + 1) * HEAD_WIDTH]
            s = dot_t(q_s[g], k)
            parts = []
            for b in range(count):
                part = s[:, b * ROWS : (b + 1) * ROWS]
                at = start + 2 * b
                lane = lax.broadcasted_iota(jnp.int32, (8, ROWS), 1)
                bias = jnp.where(lane < HALF, bias_ref[at], bias_ref[at + 1])
                part = part + bias[0:1]
                if index in diagonals and b == 0:
                    row = lax.broadcasted_iota(jnp.int32, (rows, ROWS), 0) & (ROWS - 1)
                    col = lax.broadcasted_iota(jnp.int32, (rows, ROWS), 1)
                    after = (col < HALF) & (col + diagonals[index] > row)
                    part = jnp.where(after, hidden_logits, part)
                parts.append(part)
            best = functools.reduce(jnp.maximum, parts)
            m_old = m_s[g]
            m_new = jnp.maximum(m_old, jnp.max(best, axis=1, keepdims=True))
            decay = jnp.exp2((m_old - m_new) * factor)
            m_s[g] = m_new
            scaled = m_new * factor
            weights = [jnp.exp2(part * factor - scaled) for part in parts]
            l_s[g] = l_s[g] * decay + functools.reduce(jnp.add, weights)
            p = jnp.concatenate([w.astype(BF16) for w in weights], axis=1)
            acc_s[g] = acc_s[g] * decay + dot(p, v)

    start = offset
    for index, piece in enumerate(pieces):
        if index in diagonals:
            update(index, piece, start)
        else:
            seen = bias_ref[start]
            for b in range(1, 2 * sizes[index]):
                seen = jnp.maximum(seen, bias_ref[start + b])

            @pl.when(seen > -1.0)
            def _(index=index, piece=piece, start=start):
                update(index, piece, start)

        start += 2 * sizes[index]

    if last:
        for i in range(HEADS):
            g, a = divmod(i, per_group)
            at = slice(a * ROWS, (a + 1) * ROWS)
            total = jnp.sum(l_s[g, at, :], axis=1, keepdims=True)
            o_ref[:, i * HEAD_WIDTH : (i + 1) * HEAD_WIDTH] = (acc_s[g, at, :] / total).astype(BF16)


def attend(bias, offset, queries, pieces, state=None, diagonals=(), last=False):
    sizes = tuple(piece.shape[0] // ROWS for piece in pieces)
    shape = (GROUPS, HEADS // GROUPS * ROWS, HEAD_WIDTH)
    part = jax.ShapeDtypeStruct(shape, F32)
    state = state or ()
    blocks = sum(sizes)
    scratch = [pltpu.VMEM(shape, F32)] * 3 if last else []
    return pl.pallas_call(
        functools.partial(attention_kernel, sizes, dict(diagonals), offset, not state, last),
        in_specs=[pl.BlockSpec(memory_space=pltpu.SMEM)]
        + [pl.BlockSpec(memory_space=pltpu.VMEM)] * (1 + len(pieces) + len(state)),
        out_shape=jax.ShapeDtypeStruct((ROWS, WIDTH), BF16) if last else [part] * 3,
        scratch_shapes=scratch + [pltpu.VMEM(shape, BF16)],
        compiler_params=params(24),
        cost_estimate=pl.CostEstimate(
            flops=blocks * 2**27, bytes_accessed=blocks * 2**17, transcendentals=blocks * 2**17
        ),
        name="attention",
    )(bias, queries, *pieces, *state)


def shifted(z_count, x_count, dz=0, dx=0, swap=False):
    pairs = []
    for z in range(z_count):
        for x in range(x_count):
            for c in range(2):
                s = 2 * c - 1
                source = ((z + s * dz) % z_count, (x + s * dx) % x_count, 1 - c if swap else c)
                pairs.append((place_of(z_count, x_count, *source), place_of(z_count, x_count, z, x, c)))
    return pairs


def place_of(z_count, x_count, z, x, c):
    return (z % z_count * x_count + x % x_count) * 2 + c


ZS, XS = 8, 4


def at(z, x, c):
    return place_of(ZS, XS, z, x, c)


def low_half(z, x, c):
    s = 2 * c - 1
    ids = [at(z, x, c)]
    for d in (1, 2, 3):
        ids += [at(z + d * s, x, c), at(z + d * s, x, 1 - c)]
    return ids + [at(z + 4 * s, x, c)]


def low_full(z, x, c):
    return low_half(z, x, c) + low_half(z, x, 1 - c)


def high_half(z, x, c):
    s = 2 * c - 1
    return [at(z, x, c), at(z, x + s, c), at(z, x + s, 1 - c), at(z, x + 2 * s, c)]


def high_full(z, x, c):
    return high_half(z, x, c) + high_half(z, x, 1 - c)


CALLS = (40, 48, 40)


def block_order(z, x, c):
    s = 2 * c - 1
    first = low_full(z, x, c) + high_full(z, x, c)
    first += high_full(z + s, x, c) + high_full(z - s, x, 1 - c)
    second = high_full(z + 2 * s, x, c) + high_full(z - 2 * s, x, 1 - c)
    second += low_full(z, x + s, c) + low_full(z, x - s, 1 - c)
    third = high_full(z + 3 * s, x, c) + high_full(z - 3 * s, x, 1 - c)
    third += high_half(z + 4 * s, x, c) + high_half(z - 4 * s, x, 1 - c)
    third += low_half(z, x + 2 * s, c) + low_half(z, x - 2 * s, 1 - c)
    assert (len(first), len(second), len(third)) == CALLS
    return first + second + third


def visibility():
    order = [block_order(z, x, c) for z in range(ZS) for x in range(XS) for c in range(2)]
    visible = np.array(order) <= np.arange(EXPERTS)[:, None]
    return np.where(visible, 0.0, hidden_logits).astype(np.float32)


def attention(place, queries, own, beside):
    along_z = lambda v: lax.ppermute(v, "exp", shifted(ZS, XS, dz=1))
    along_x = lambda v: lax.ppermute(v, "exp", shifted(ZS, XS, dx=1))
    swap = lambda v: lax.ppermute(v, "exp", shifted(ZS, XS, swap=True))
    tie = lax.optimization_barrier
    bias = lax.dynamic_index_in_dim(jnp.asarray(visibility()), place, 0, keepdims=False)

    other = swap(own)
    low1 = along_z(jnp.concatenate([own[:HALF], other[:HALF]]))
    high1 = along_x(jnp.concatenate([own[HALF:], other[HALF:]]))
    low1, high1 = tie((low1, high1))
    low2 = along_z(low1)
    high2 = along_x(high1[:HALF])
    low2, high2 = tie((low2, high2))
    low3 = along_z(low2)
    half_high = jnp.concatenate([own[HALF:], high1, high2])
    full_high = jnp.concatenate([half_high, swap(half_high)])
    z1 = along_z(full_high)
    low3_lead, z1 = tie((low3[:HALF], z1))
    low4 = along_z(low3_lead)
    half_low = jnp.concatenate([own[:HALF], low1, low2, low3, low4])
    full_low = jnp.concatenate([half_low, swap(half_low)])
    x1 = along_x(full_low)
    z2 = along_z(z1)
    state = attend(
        bias,
        0,
        queries,
        [full_low, full_high, z1, swap(z1)],
        diagonals=((0, 0), (1, HALF)),
    )
    z2, top = tie((z2, state[0]))
    x1, total, sums = tie((x1, state[1], state[2]))
    z3 = along_z(z2)
    x2 = along_x(x1[: half_low.shape[0]])
    z4 = along_z(z3[: half_high.shape[0]])
    state = attend(
        bias, CALLS[0], queries, [z2, swap(z2), x1, swap(x1)], (top, total, sums)
    )
    z4, top = tie((z4, state[0]))
    x2, total, sums, beside = tie((x2, state[1], state[2], beside))
    attended = attend(
        bias,
        CALLS[0] + CALLS[1],
        queries,
        [z3, swap(z3), z4, swap(z4), x2, swap(x2)],
        (top, total, sums),
        last=True,
    )
    return attended, beside


def pieces_of(values):
    return [values[:, j * PIECE : (j + 1) * PIECE] for j in range(PIECES)]


def send_kernel(picker_ref, rows_ref, spread_ref, o_ref):
    for b in range(BUNCHES):
        picked = dot(picker_ref[b * COMPACT : (b + 1) * COMPACT, :], rows_ref[...]).astype(BF16)
        out = sum(dot(spread_ref[j], part) for j, part in enumerate(pieces_of(picked)))
        o_ref[b * SPREAD : (b + 1) * SPREAD, :] = out.astype(BF16)


def send_rows(picker, rows, spread):
    return pl.pallas_call(
        send_kernel,
        out_shape=jax.ShapeDtypeStruct((PLACES * PIECES, PIECE), BF16),
        compiler_params=params(14),
        name="send_rows",
    )(picker, rows, spread)


def gather_compact(source_ref, gather_ref, target_ref):
    for b in range(BUNCHES):
        part = source_ref[b * SPREAD : (b + 1) * SPREAD, :]
        for j in range(PIECES):
            target_ref[b * COMPACT : (b + 1) * COMPACT, j * PIECE : (j + 1) * PIECE] = dot(
                gather_ref[j], part
            ).astype(BF16)


TILE = 256


def high_low(x):
    high = x.astype(BF16).astype(F32)
    column = lax.broadcasted_iota(jnp.int32, (x.shape[0], 128), 1)
    return jnp.where(column == 0, high, jnp.where(column == 1, x - high, 0.0)).astype(BF16)


def first_kernel(by_rows, x_ref, gather_ref, w_ref, o_ref, compact_ref, squares_ref):
    @pl.when(pl.program_id(0) == 0)
    def _():
        gather_compact(x_ref, gather_ref, compact_ref)
        for b in range(BUNCHES):
            rows = compact_ref[b * COMPACT : (b + 1) * COMPACT, :].astype(F32)
            squares_ref[b * COMPACT : (b + 1) * COMPACT, :] = high_low(
                jnp.sum(rows * rows, axis=1, keepdims=True)
            )

    product = dot_t if by_rows else dot
    o_ref[...] = product(compact_ref[...], w_ref[...]).astype(BF16)


def first_product(x, gather, w, by_rows):
    if by_rows:
        outs = w.shape[0]
        w_spec = pl.BlockSpec((TILE, WIDTH), lambda i: (i, 0))
    else:
        outs = w.shape[1]
        w_spec = pl.BlockSpec((WIDTH, TILE), lambda i: (0, i))
    return pl.pallas_call(
        functools.partial(first_kernel, by_rows),
        grid=(outs // TILE,),
        in_specs=[
            pl.BlockSpec(x.shape, lambda i: (0, 0)),
            pl.BlockSpec(gather.shape, lambda i: (0, 0, 0)),
            w_spec,
        ],
        out_specs=[
            pl.BlockSpec((PLACES, TILE), lambda i: (0, i)),
            pl.BlockSpec((PLACES, WIDTH), lambda i: (0, 0)),
            pl.BlockSpec((PLACES, 128), lambda i: (0, 0)),
        ],
        out_shape=[
            jax.ShapeDtypeStruct((PLACES, outs), BF16),
            jax.ShapeDtypeStruct((PLACES, WIDTH), BF16),
            jax.ShapeDtypeStruct((PLACES, 128), BF16),
        ],
        compiler_params=params(22),
        name="first_product",
    )(x, gather, w)


def second_kernel(by_rows, corrected, head_ref, *refs):
    pieces, refs = refs[:HEAD_COUNT], refs[HEAD_COUNT:]
    if corrected:
        w_ref, spread_ref, row_ref, o_ref, h_s, y_s, weight_s = refs
    else:
        w_ref, spread_ref, o_ref, h_s, y_s = refs
    step = pl.program_id(0)
    depth = h_s.shape[1]
    quarter = PLACES // HEAD_COUNT

    @pl.when(step == 0)
    def _():
        for d, piece in enumerate(pieces):
            at = lax.rem(head_ref[0] + d, HEAD_COUNT) * quarter
            at = pl.ds(pl.multiple_of(at, 16), quarter)
            h_s[at, :] = piece[:, :depth]
            if corrected:
                weight_s[at, :] = piece[:, depth : depth + 128].astype(F32)

    product = dot_t if by_rows else dot
    y = product(h_s[...], w_ref[...])
    if corrected:
        y = y - row_ref[...].astype(F32) * (weight_s[:, 0:1] + weight_s[:, 1:2])
    y_s[step] = y.astype(BF16)

    @pl.when(step == PIECES - 1)
    def _():
        for b in range(BUNCHES):
            out = sum(
                dot(spread_ref[j], y_s[j, b * COMPACT : (b + 1) * COMPACT, :]) for j in range(PIECES)
            )
            o_ref[b * SPREAD : (b + 1) * SPREAD, :] = out.astype(BF16)


def second_product(head, pieces, w, spread, by_rows, rows=None):
    depth = w.shape[1] if by_rows else w.shape[0]
    w_spec = (
        pl.BlockSpec((PIECE, depth), lambda i, s: (i, 0))
        if by_rows
        else pl.BlockSpec((depth, PIECE), lambda i, s: (0, i))
    )
    in_specs = [pl.BlockSpec(piece.shape, lambda i, s: (0, 0)) for piece in pieces] + [
        w_spec,
        pl.BlockSpec(spread.shape, lambda i, s: (0, 0, 0)),
    ]
    args = [*pieces, w, spread]
    scratch = [pltpu.VMEM((PLACES, depth), BF16), pltpu.VMEM((PIECES, PLACES, PIECE), BF16)]
    if rows is not None:
        in_specs += [pl.BlockSpec((PLACES, PIECE), lambda i, s: (0, i))]
        args += [rows]
        scratch += [pltpu.VMEM((PLACES, 128), F32)]
    return pl.pallas_call(
        functools.partial(second_kernel, by_rows, rows is not None),
        grid_spec=pltpu.PrefetchScalarGridSpec(
            num_scalar_prefetch=1,
            grid=(PIECES,),
            in_specs=in_specs,
            out_specs=pl.BlockSpec((PLACES * PIECES, PIECE), lambda i, s: (0, 0)),
            scratch_shapes=scratch,
        ),
        out_shape=jax.ShapeDtypeStruct((PLACES * PIECES, PIECE), BF16),
        compiler_params=params(32),
        name="second_product",
    )(head[None], *args)


def combine_kernel(came_ref, gather_ref, weight_ref, base_ref, o_ref, compact_s):
    gather_compact(came_ref, gather_ref, compact_s)
    both = dot(weight_ref[...], compact_s[...])
    o_ref[...] = (base_ref[...].astype(F32) + (both[:ROWS] + both[ROWS:])).astype(BF16)


def combine(came, gather, weight, base):
    return pl.pallas_call(
        combine_kernel,
        out_shape=jax.ShapeDtypeStruct((ROWS, WIDTH), BF16),
        scratch_shapes=[pltpu.VMEM((PLACES, WIDTH), BF16)],
        compiler_params=params(18),
        name="combine",
    )(came, gather, weight, base)


def exchange(x):
    y = lax.all_to_all(
        x.reshape(EXPERTS, CAP * PIECES, PIECE), "exp", split_axis=0, concat_axis=0, tiled=True
    )
    return y.reshape(PLACES * PIECES, PIECE)


def up(x):
    return lax.ppermute(x, "head", [(i, (i + 1) % HEAD_COUNT) for i in range(HEAD_COUNT)])


def down(x):
    return lax.ppermute(x, "head", [(i, (i - 1) % HEAD_COUNT) for i in range(HEAD_COUNT)])


def head_scatter(head, x, squares=None):
    width = x.shape[1]
    if squares is not None:
        x = jnp.concatenate([x, squares], axis=1)
    rows = x.shape[0] // HEAD_COUNT
    half = rows // 2

    def part(d, at, count):
        return lax.dynamic_slice_in_dim(x, (head + d) % HEAD_COUNT * rows + at, count)

    def plus(a, b):
        total = a[:, :width].astype(F32) + b[:, :width].astype(F32)
        if squares is None:
            return total.astype(BF16)
        column = column_of(a) + column_of(b)
        return jnp.concatenate([total.astype(BF16), high_low(column)], axis=1)

    def column_of(a):
        return a[:, width : width + 1].astype(F32) + a[:, width + 1 : width + 2].astype(F32)

    low = up(jnp.concatenate([part(2, 0, half), part(1, half, half)]))
    high = down(jnp.concatenate([part(2, half, half), part(-1, 0, half)]))
    low2 = up(plus(part(1, 0, half), low[:half]))
    high2 = down(plus(part(-1, half, half), high[:half]))
    own = part(0, 0, rows)

    def total(f):
        return f(own) + jnp.concatenate([f(low2) + f(high[half:]), f(low[half:]) + f(high2)])

    sums = total(lambda a: a[:, :width].astype(F32))
    return sums if squares is None else (sums, total(column_of))


def head_gather(x):
    half = x.shape[0] // 2
    low = up(x)
    high = down(x)
    opposite = jnp.concatenate([up(low[:half]), down(high[half:])])
    return [x, high, opposite, low]


def per_device(queries, keys, values, w_in, w_out, routes, route_weights, grad_out):
    place = lax.axis_index("exp").astype(jnp.int32)
    head = lax.axis_index("head").astype(jnp.int32)
    w_first = w_in[0].reshape(WIDTH, 2 * FF)
    w_second = w_out[0]
    matrix = spread_matrix()
    spread = jnp.asarray(matrix, BF16)
    gather = jnp.asarray(matrix.transpose(0, 2, 1), BF16)

    hits = routes[:, :, None] == jnp.arange(EXPERTS, dtype=jnp.int32)
    hit = jnp.any(hits, axis=1)
    earlier = jnp.asarray(np.tril(np.ones((ROWS, ROWS), np.float32), -1), BF16)
    rank = dot(earlier, hit.astype(BF16))
    rank = jnp.where(hit, rank, -1.0)
    token_weight = jnp.sum(jnp.where(hits, route_weights[:, :, None], 0.0), axis=1)
    slots = jnp.arange(CAP, dtype=jnp.int32).astype(F32)
    picker = (rank.T[:, None, :] == slots[None, :, None]).astype(BF16).reshape(PLACES, ROWS)
    weight = jnp.where(rank[:, :, None] == slots, token_weight[:, :, None], 0.0).reshape(ROWS, PLACES)
    weight_high = weight.astype(BF16)
    weight_low = (weight - weight_high.astype(F32)).astype(BF16)
    weight_both = jnp.concatenate([weight_high, weight_low], axis=0)

    grads_in = exchange(send_rows(picker, grad_out, spread))
    back, _, _ = first_product(grads_in, gather, w_second, True)
    attended, back = attention(place, queries, jnp.concatenate([keys, values], axis=1), back)
    back = head_scatter(head, back)

    rows_in = exchange(send_rows(picker, attended, spread))
    rows_in, back, weight_both = lax.optimization_barrier((rows_in, back, weight_both))
    raw, rows, squares = first_product(rows_in, gather, w_first, False)
    raw, squares = head_scatter(head, raw, squares)
    scale = lax.rsqrt(squares / D + norm_eps)
    gate = raw[:, :FF] * scale
    lift = raw[:, FF:] * scale
    sigmoid = jax.nn.sigmoid(gate)
    silu = gate * sigmoid
    act = (silu * lift).astype(BF16)
    grad_gate = (back * lift * sigmoid * (1.0 + gate * (1.0 - sigmoid)) * scale).astype(BF16)
    grad_up = (back * silu * scale).astype(BF16)
    inner = jnp.sum(
        grad_gate.astype(F32) * gate + grad_up.astype(F32) * lift, axis=1, keepdims=True
    )
    correction = high_low(inner * scale / D)
    gathered = head_gather(act)
    came_out = exchange(second_product(head, gathered, w_second, spread, False))
    grad_hidden = head_gather(jnp.concatenate([grad_gate, grad_up, correction], axis=1))
    came_grad = exchange(second_product(head, grad_hidden, w_first, spread, True, rows))
    output = combine(came_out, gather, weight_both, attended)
    grad_attended = combine(came_grad, gather, weight_both, grad_out)
    return (output, grad_attended)


def solution(mesh):
    in_specs = (
        P("exp", "head"),
        P("exp", "head"),
        P("exp", "head"),
        P("exp", "head", None, None),
        P("exp", None, "head"),
        P("exp", None),
        P("exp", None),
        P("exp", "head"),
    )
    out_specs = (P("exp", "head"), P("exp", "head"))
    return jax.shard_map(
        per_device, mesh=mesh, in_specs=in_specs, out_specs=out_specs, check_vma=False
    )
```

```python
import functools

import jax
import jax.numpy as jnp
import numpy as np
from jax import lax
from jax.experimental import pallas as pl
from jax.experimental.pallas import tpu as pltpu
from jax.sharding import PartitionSpec as P

D = 4096
HEAD_WIDTH = 128
TOP = 6
norm_eps = 1e-05
hidden_logits = -1e30

ROWS = 128
HALF = ROWS // 2
HEADS = 8
GROUPS = 2
WIDTH = 1024
FF = 768
EXPERTS = 64
HEAD_COUNT = 4
CAP = 14
PIECES = 4
PIECE = WIDTH // PIECES
BUNCH = 8
COMPACT = BUNCH * CAP
SPREAD = BUNCH * CAP * PIECES
BUNCHES = EXPERTS // BUNCH
PLACES = EXPERTS * CAP
F32 = jnp.float32
BF16 = jnp.bfloat16
MIB = 1 << 20


def params(mib):
    return pltpu.CompilerParams(vmem_limit_bytes=mib * MIB)


def spread_matrix():
    spread = np.arange(SPREAD)
    compact = np.arange(COMPACT)
    source = spread // (CAP * PIECES) * CAP + spread % CAP
    piece = spread % (CAP * PIECES) // CAP
    same = source[:, None] == compact[None, :]
    return np.stack([same & (piece[:, None] == j) for j in range(PIECES)]).astype(np.float32)


def dot(a, b):
    return lax.dot_general(a, b, (((1,), (0,)), ((), ())), preferred_element_type=F32)


def dot_t(a, b):
    return lax.dot_general(a, b, (((1,), (1,)), ((), ())), preferred_element_type=F32)


def attention_kernel(sizes, diagonals, offset, first, last, *refs):
    refs = list(refs)
    bias_ref, q_ref = refs[:2]
    pieces = refs[2 : 2 + len(sizes)]
    rest = refs[2 + len(sizes) :]
    if not first:
        olds, rest = rest[:3], rest[3:]
    if last:
        o_ref, rest = rest[0], rest[1:]
    m_s, l_s, acc_s, q_s = rest
    per_group = HEADS // GROUPS
    rows = per_group * ROWS
    factor = HEAD_WIDTH**-0.5 * 1.4426950408889634
    for i in range(HEADS):
        g, a = divmod(i, per_group)
        q_s[g, a * ROWS : (a + 1) * ROWS, :] = q_ref[:, i * HEAD_WIDTH : (i + 1) * HEAD_WIDTH]
    if first:
        m_s[...] = jnp.full(m_s.shape, hidden_logits, F32)
        l_s[...] = jnp.zeros(l_s.shape, F32)
        acc_s[...] = jnp.zeros(acc_s.shape, F32)
    else:
        m_s[...] = olds[0][...]
        l_s[...] = olds[1][...]
        acc_s[...] = olds[2][...]

    def update(index, kv_ref, start):
        count = sizes[index]
        for g in range(GROUPS):
            k = kv_ref[:, g * HEAD_WIDTH : (g + 1) * HEAD_WIDTH]
            v = kv_ref[:, (GROUPS + g) * HEAD_WIDTH : (GROUPS + g + 1) * HEAD_WIDTH]
            s = dot_t(q_s[g], k)
            parts = []
            for b in range(count):
                part = s[:, b * ROWS : (b + 1) * ROWS]
                at = start + 2 * b
                lane = lax.broadcasted_iota(jnp.int32, (8, ROWS), 1)
                bias = jnp.where(lane < HALF, bias_ref[at], bias_ref[at + 1])
                part = part + bias[0:1]
                if index in diagonals and b == 0:
                    row = lax.broadcasted_iota(jnp.int32, (rows, ROWS), 0) & (ROWS - 1)
                    col = lax.broadcasted_iota(jnp.int32, (rows, ROWS), 1)
                    after = (col < HALF) & (col + diagonals[index] > row)
                    part = jnp.where(after, hidden_logits, part)
                parts.append(part)
            best = functools.reduce(jnp.maximum, parts)
            m_old = m_s[g]
            m_new = jnp.maximum(m_old, jnp.max(best, axis=1, keepdims=True))
            decay = jnp.exp2((m_old - m_new) * factor)
            m_s[g] = m_new
            scaled = m_new * factor
            weights = [jnp.exp2(part * factor - scaled) for part in parts]
            l_s[g] = l_s[g] * decay + functools.reduce(jnp.add, weights)
            p = jnp.concatenate([w.astype(BF16) for w in weights], axis=1)
            acc_s[g] = acc_s[g] * decay + dot(p, v)

    start = offset
    for index, piece in enumerate(pieces):
        if index in diagonals:
            update(index, piece, start)
        else:
            seen = bias_ref[start]
            for b in range(1, 2 * sizes[index]):
                seen = jnp.maximum(seen, bias_ref[start + b])

            @pl.when(seen > -1.0)
            def _(index=index, piece=piece, start=start):
                update(index, piece, start)

        start += 2 * sizes[index]

    if last:
        for i in range(HEADS):
            g, a = divmod(i, per_group)
            at = slice(a * ROWS, (a + 1) * ROWS)
            total = jnp.sum(l_s[g, at, :], axis=1, keepdims=True)
            o_ref[:, i * HEAD_WIDTH : (i + 1) * HEAD_WIDTH] = (acc_s[g, at, :] / total).astype(BF16)


def attend(bias, offset, queries, pieces, state=None, diagonals=(), last=False):
    sizes = tuple(piece.shape[0] // ROWS for piece in pieces)
    shape = (GROUPS, HEADS // GROUPS * ROWS, HEAD_WIDTH)
    part = jax.ShapeDtypeStruct(shape, F32)
    state = state or ()
    blocks = sum(sizes)
    scratch = [pltpu.VMEM(shape, F32)] * 3 if last else []
    return pl.pallas_call(
        functools.partial(attention_kernel, sizes, dict(diagonals), offset, not state, last),
        in_specs=[pl.BlockSpec(memory_space=pltpu.SMEM)]
        + [pl.BlockSpec(memory_space=pltpu.VMEM)] * (1 + len(pieces) + len(state)),
        out_shape=jax.ShapeDtypeStruct((ROWS, WIDTH), BF16) if last else [part] * 3,
        scratch_shapes=scratch + [pltpu.VMEM(shape, BF16)],
        compiler_params=params(24),
        cost_estimate=pl.CostEstimate(
            flops=blocks * 2**27, bytes_accessed=blocks * 2**17, transcendentals=blocks * 2**17
        ),
        name="attention",
    )(bias, queries, *pieces, *state)


def shifted(z_count, x_count, dz=0, dx=0, swap=False):
    pairs = []
    for z in range(z_count):
        for x in range(x_count):
            for c in range(2):
                s = 2 * c - 1
                source = ((z + s * dz) % z_count, (x + s * dx) % x_count, 1 - c if swap else c)
                pairs.append((place_of(z_count, x_count, *source), place_of(z_count, x_count, z, x, c)))
    return pairs


def place_of(z_count, x_count, z, x, c):
    return (z % z_count * x_count + x % x_count) * 2 + c


ZS, XS = 8, 4


def at(z, x, c):
    return place_of(ZS, XS, z, x, c)


def low_half(z, x, c):
    s = 2 * c - 1
    ids = [at(z, x, c)]
    for d in (1, 2, 3):
        ids += [at(z + d * s, x, c), at(z + d * s, x, 1 - c)]
    return ids + [at(z + 4 * s, x, c)]


def low_full(z, x, c):
    return low_half(z, x, c) + low_half(z, x, 1 - c)


def high_half(z, x, c):
    s = 2 * c - 1
    return [at(z, x, c), at(z, x + s, c), at(z, x + s, 1 - c), at(z, x + 2 * s, c)]


def high_full(z, x, c):
    return high_half(z, x, c) + high_half(z, x, 1 - c)


CALLS = (40, 48, 40)


def block_order(z, x, c):
    s = 2 * c - 1
    first = low_full(z, x, c) + high_full(z, x, c)
    first += high_full(z + s, x, c) + high_full(z - s, x, 1 - c)
    second = high_full(z + 2 * s, x, c) + high_full(z - 2 * s, x, 1 - c)
    second += low_full(z, x + s, c) + low_full(z, x - s, 1 - c)
    third = high_full(z + 3 * s, x, c) + high_full(z - 3 * s, x, 1 - c)
    third += high_half(z + 4 * s, x, c) + high_half(z - 4 * s, x, 1 - c)
    third += low_half(z, x + 2 * s, c) + low_half(z, x - 2 * s, 1 - c)
    assert (len(first), len(second), len(third)) == CALLS
    return first + second + third


def visibility():
    order = [block_order(z, x, c) for z in range(ZS) for x in range(XS) for c in range(2)]
    visible = np.array(order) <= np.arange(EXPERTS)[:, None]
    return np.where(visible, 0.0, hidden_logits).astype(np.float32)


def attention(place, queries, own):
    along_z = lambda v: lax.ppermute(v, "exp", shifted(ZS, XS, dz=1))
    along_x = lambda v: lax.ppermute(v, "exp", shifted(ZS, XS, dx=1))
    swap = lambda v: lax.ppermute(v, "exp", shifted(ZS, XS, swap=True))
    tie = lax.optimization_barrier
    bias = lax.dynamic_index_in_dim(jnp.asarray(visibility()), place, 0, keepdims=False)

    other = swap(own)
    low1 = along_z(jnp.concatenate([own[:HALF], other[:HALF]]))
    high1 = along_x(jnp.concatenate([own[HALF:], other[HALF:]]))
    low1, high1 = tie((low1, high1))
    low2 = along_z(low1)
    high2 = along_x(high1[:HALF])
    low2, high2 = tie((low2, high2))
    low3 = along_z(low2)
    half_high = jnp.concatenate([own[HALF:], high1, high2])
    full_high = jnp.concatenate([half_high, swap(half_high)])
    z1 = along_z(full_high)
    low3_lead, z1 = tie((low3[:HALF], z1))
    low4 = along_z(low3_lead)
    half_low = jnp.concatenate([own[:HALF], low1, low2, low3, low4])
    full_low = jnp.concatenate([half_low, swap(half_low)])
    x1 = along_x(full_low)
    z2 = along_z(z1)
    state = attend(
        bias,
        0,
        queries,
        [full_low, full_high, z1, swap(z1)],
        diagonals=((0, 0), (1, HALF)),
    )
    z2, top = tie((z2, state[0]))
    x1, total, sums = tie((x1, state[1], state[2]))
    z3 = along_z(z2)
    x2 = along_x(x1[: half_low.shape[0]])
    z4 = along_z(z3[: half_high.shape[0]])
    state = attend(
        bias, CALLS[0], queries, [z2, swap(z2), x1, swap(x1)], (top, total, sums)
    )
    z4, top = tie((z4, state[0]))
    x2, total, sums = tie((x2, state[1], state[2]))
    return attend(
        bias,
        CALLS[0] + CALLS[1],
        queries,
        [z3, swap(z3), z4, swap(z4), x2, swap(x2)],
        (top, total, sums),
        last=True,
    )


def pieces_of(values):
    return [values[:, j * PIECE : (j + 1) * PIECE] for j in range(PIECES)]


def send_kernel(picker_ref, rows_ref, spread_ref, o_ref):
    for b in range(BUNCHES):
        picked = dot(picker_ref[b * COMPACT : (b + 1) * COMPACT, :], rows_ref[...]).astype(BF16)
        out = sum(dot(spread_ref[j], part) for j, part in enumerate(pieces_of(picked)))
        o_ref[b * SPREAD : (b + 1) * SPREAD, :] = out.astype(BF16)


def send_rows(picker, rows, spread):
    return pl.pallas_call(
        send_kernel,
        out_shape=jax.ShapeDtypeStruct((PLACES * PIECES, PIECE), BF16),
        compiler_params=params(14),
        name="send_rows",
    )(picker, rows, spread)


def gather_compact(source_ref, gather_ref, target_ref):
    for b in range(BUNCHES):
        part = source_ref[b * SPREAD : (b + 1) * SPREAD, :]
        for j in range(PIECES):
            target_ref[b * COMPACT : (b + 1) * COMPACT, j * PIECE : (j + 1) * PIECE] = dot(
                gather_ref[j], part
            ).astype(BF16)


TILE = 256


def high_low(x):
    high = x.astype(BF16).astype(F32)
    column = lax.broadcasted_iota(jnp.int32, (x.shape[0], 128), 1)
    return jnp.where(column == 0, high, jnp.where(column == 1, x - high, 0.0)).astype(BF16)


def first_kernel(by_rows, x_ref, gather_ref, w_ref, o_ref, compact_ref, squares_ref):
    @pl.when(pl.program_id(0) == 0)
    def _():
        gather_compact(x_ref, gather_ref, compact_ref)
        for b in range(BUNCHES):
            rows = compact_ref[b * COMPACT : (b + 1) * COMPACT, :].astype(F32)
            squares_ref[b * COMPACT : (b + 1) * COMPACT, :] = high_low(
                jnp.sum(rows * rows, axis=1, keepdims=True)
            )

    product = dot_t if by_rows else dot
    o_ref[...] = product(compact_ref[...], w_ref[...]).astype(BF16)


def first_product(x, gather, w, by_rows):
    if by_rows:
        outs = w.shape[0]
        w_spec = pl.BlockSpec((TILE, WIDTH), lambda i: (i, 0))
    else:
        outs = w.shape[1]
        w_spec = pl.BlockSpec((WIDTH, TILE), lambda i: (0, i))
    return pl.pallas_call(
        functools.partial(first_kernel, by_rows),
        grid=(outs // TILE,),
        in_specs=[
            pl.BlockSpec(x.shape, lambda i: (0, 0)),
            pl.BlockSpec(gather.shape, lambda i: (0, 0, 0)),
            w_spec,
        ],
        out_specs=[
            pl.BlockSpec((PLACES, TILE), lambda i: (0, i)),
            pl.BlockSpec((PLACES, WIDTH), lambda i: (0, 0)),
            pl.BlockSpec((PLACES, 128), lambda i: (0, 0)),
        ],
        out_shape=[
            jax.ShapeDtypeStruct((PLACES, outs), BF16),
            jax.ShapeDtypeStruct((PLACES, WIDTH), BF16),
            jax.ShapeDtypeStruct((PLACES, 128), BF16),
        ],
        compiler_params=params(22),
        name="first_product",
    )(x, gather, w)


def second_kernel(by_rows, corrected, head_ref, *refs):
    pieces, refs = refs[:HEAD_COUNT], refs[HEAD_COUNT:]
    if corrected:
        w_ref, spread_ref, row_ref, o_ref, h_s, y_s, weight_s = refs
    else:
        w_ref, spread_ref, o_ref, h_s, y_s = refs
    step = pl.program_id(0)
    depth = h_s.shape[1]
    quarter = PLACES // HEAD_COUNT

    @pl.when(step == 0)
    def _():
        for d, piece in enumerate(pieces):
            at = lax.rem(head_ref[0] + d, HEAD_COUNT) * quarter
            at = pl.ds(pl.multiple_of(at, 16), quarter)
            h_s[at, :] = piece[:, :depth]
            if corrected:
                weight_s[at, :] = piece[:, depth : depth + 128].astype(F32)

    product = dot_t if by_rows else dot
    y = product(h_s[...], w_ref[...])
    if corrected:
        y = y - row_ref[...].astype(F32) * (weight_s[:, 0:1] + weight_s[:, 1:2])
    y_s[step] = y.astype(BF16)

    @pl.when(step == PIECES - 1)
    def _():
        for b in range(BUNCHES):
            out = sum(
                dot(spread_ref[j], y_s[j, b * COMPACT : (b + 1) * COMPACT, :]) for j in range(PIECES)
            )
            o_ref[b * SPREAD : (b + 1) * SPREAD, :] = out.astype(BF16)


def second_product(head, pieces, w, spread, by_rows, rows=None):
    depth = w.shape[1] if by_rows else w.shape[0]
    w_spec = (
        pl.BlockSpec((PIECE, depth), lambda i, s: (i, 0))
        if by_rows
        else pl.BlockSpec((depth, PIECE), lambda i, s: (0, i))
    )
    in_specs = [pl.BlockSpec(piece.shape, lambda i, s: (0, 0)) for piece in pieces] + [
        w_spec,
        pl.BlockSpec(spread.shape, lambda i, s: (0, 0, 0)),
    ]
    args = [*pieces, w, spread]
    scratch = [pltpu.VMEM((PLACES, depth), BF16), pltpu.VMEM((PIECES, PLACES, PIECE), BF16)]
    if rows is not None:
        in_specs += [pl.BlockSpec((PLACES, PIECE), lambda i, s: (0, i))]
        args += [rows]
        scratch += [pltpu.VMEM((PLACES, 128), F32)]
    return pl.pallas_call(
        functools.partial(second_kernel, by_rows, rows is not None),
        grid_spec=pltpu.PrefetchScalarGridSpec(
            num_scalar_prefetch=1,
            grid=(PIECES,),
            in_specs=in_specs,
            out_specs=pl.BlockSpec((PLACES * PIECES, PIECE), lambda i, s: (0, 0)),
            scratch_shapes=scratch,
        ),
        out_shape=jax.ShapeDtypeStruct((PLACES * PIECES, PIECE), BF16),
        compiler_params=params(32),
        name="second_product",
    )(head[None], *args)


def combine_kernel(came_ref, gather_ref, weight_ref, base_ref, o_ref, compact_s):
    gather_compact(came_ref, gather_ref, compact_s)
    both = dot(weight_ref[...], compact_s[...])
    o_ref[...] = (base_ref[...].astype(F32) + (both[:ROWS] + both[ROWS:])).astype(BF16)


def combine(came, gather, weight, base):
    return pl.pallas_call(
        combine_kernel,
        out_shape=jax.ShapeDtypeStruct((ROWS, WIDTH), BF16),
        scratch_shapes=[pltpu.VMEM((PLACES, WIDTH), BF16)],
        compiler_params=params(18),
        name="combine",
    )(came, gather, weight, base)


def exchange(x):
    y = lax.all_to_all(
        x.reshape(EXPERTS, CAP * PIECES, PIECE), "exp", split_axis=0, concat_axis=0, tiled=True
    )
    return y.reshape(PLACES * PIECES, PIECE)


def from_head(x, d):
    return lax.ppermute(x, "head", [((i + d) % HEAD_COUNT, i) for i in range(HEAD_COUNT)])


OTHERS = (1, 3, 2)


def head_scatter(head, x):
    rows = x.shape[0] // HEAD_COUNT

    def part(d):
        return lax.dynamic_slice_in_dim(x, (head + d) % HEAD_COUNT * rows, rows)

    return [part(0)] + [from_head(part(-d), d) for d in OTHERS]


def head_gather(x):
    parts = {d: from_head(x, d) for d in OTHERS}
    return [x] + [parts[d] for d in range(1, HEAD_COUNT)]


def total(parts):
    return functools.reduce(jnp.add, [part.astype(F32) for part in parts])


def per_device(queries, keys, values, w_in, w_out, routes, route_weights, grad_out):
    place = lax.axis_index("exp").astype(jnp.int32)
    head = lax.axis_index("head").astype(jnp.int32)
    w_first = w_in[0].reshape(WIDTH, 2 * FF)
    w_second = w_out[0]
    matrix = spread_matrix()
    spread = jnp.asarray(matrix, BF16)
    gather = jnp.asarray(matrix.transpose(0, 2, 1), BF16)

    hits = routes[:, :, None] == jnp.arange(EXPERTS, dtype=jnp.int32)
    hit = jnp.any(hits, axis=1)
    earlier = jnp.asarray(np.tril(np.ones((ROWS, ROWS), np.float32), -1), BF16)
    rank = dot(earlier, hit.astype(BF16))
    rank = jnp.where(hit, rank, -1.0)
    token_weight = jnp.sum(jnp.where(hits, route_weights[:, :, None], 0.0), axis=1)
    slots = jnp.arange(CAP, dtype=jnp.int32).astype(F32)
    picker = (rank.T[:, None, :] == slots[None, :, None]).astype(BF16).reshape(PLACES, ROWS)
    weight = jnp.where(rank[:, :, None] == slots, token_weight[:, :, None], 0.0).reshape(ROWS, PLACES)
    weight_high = weight.astype(BF16)
    weight_low = (weight - weight_high.astype(F32)).astype(BF16)
    weight_both = jnp.concatenate([weight_high, weight_low], axis=0)

    attended = attention(place, queries, jnp.concatenate([keys, values], axis=1))

    rows_in = exchange(send_rows(picker, attended, spread))
    sent_grads, weight_both, rows_in = lax.optimization_barrier(
        (send_rows(picker, grad_out, spread), weight_both, rows_in)
    )
    raw, rows, squares = first_product(rows_in, gather, w_first, False)
    sent_grads, raw = lax.optimization_barrier((sent_grads, raw))
    raw = head_scatter(head, jnp.concatenate([raw, squares], axis=1))
    grads_in = exchange(sent_grads)
    raw = total(raw)
    squares = raw[:, 2 * FF : 2 * FF + 1] + raw[:, 2 * FF + 1 : 2 * FF + 2]
    scale = lax.rsqrt(squares / D + norm_eps)
    gate = raw[:, :FF] * scale
    lift = raw[:, FF : 2 * FF] * scale
    sigmoid = jax.nn.sigmoid(gate)
    silu = gate * sigmoid
    act = (silu * lift).astype(BF16)
    gathered = head_gather(act)

    grads_in, act = lax.optimization_barrier((grads_in, act))
    back, _, _ = first_product(grads_in, gather, w_second, True)
    back = head_scatter(head, back)
    gathered[0], *back = lax.optimization_barrier((act, *back))
    back = total(back)
    grad_gate = (back * lift * sigmoid * (1.0 + gate * (1.0 - sigmoid)) * scale).astype(BF16)
    grad_up = (back * silu * scale).astype(BF16)
    inner = jnp.sum(
        grad_gate.astype(F32) * gate + grad_up.astype(F32) * lift, axis=1, keepdims=True
    )
    correction = high_low(inner * scale / D)
    came_out = exchange(second_product(head, gathered, w_second, spread, False))
    grad_hidden = head_gather(jnp.concatenate([grad_gate, grad_up, correction], axis=1))
    came_grad = exchange(second_product(head, grad_hidden, w_first, spread, True, rows))
    output = combine(came_out, gather, weight_both, attended)
    grad_attended = combine(came_grad, gather, weight_both, grad_out)
    return (output, grad_attended)


def solution(mesh):
    in_specs = (
        P("exp", "head"),
        P("exp", "head"),
        P("exp", "head"),
        P("exp", "head", None, None),
        P("exp", None, "head"),
        P("exp", None),
        P("exp", None),
        P("exp", "head"),
    )
    out_specs = (P("exp", "head"), P("exp", "head"))
    return jax.shard_map(
        per_device, mesh=mesh, in_specs=in_specs, out_specs=out_specs, check_vma=False
    )
```

```python
import functools

import jax
import jax.numpy as jnp
import numpy as np
from jax import lax
from jax.experimental import pallas as pl
from jax.experimental.pallas import tpu as pltpu
from jax.sharding import PartitionSpec as P

D = 4096
HEAD_WIDTH = 128
TOP = 6
norm_eps = 1e-05
hidden_logits = -1e30

ROWS = 128
HEADS = 8
GROUPS = 2
WIDTH = 1024
FF = 768
EXPERTS = 64
HEAD_COUNT = 4
CAP = 14
PIECES = 4
PIECE = WIDTH // PIECES
BUNCH = 8
COMPACT = BUNCH * CAP
SPREAD = BUNCH * CAP * PIECES
BUNCHES = EXPERTS // BUNCH
PLACES = EXPERTS * CAP
F32 = jnp.float32
BF16 = jnp.bfloat16
MIB = 1 << 20


def params(mib):
    return pltpu.CompilerParams(vmem_limit_bytes=mib * MIB)


def spread_matrix():
    spread = np.arange(SPREAD)
    compact = np.arange(COMPACT)
    source = spread // (CAP * PIECES) * CAP + spread % CAP
    piece = spread % (CAP * PIECES) // CAP
    same = source[:, None] == compact[None, :]
    return np.stack([same & (piece[:, None] == j) for j in range(PIECES)]).astype(np.float32)


def dot(a, b):
    return lax.dot_general(a, b, (((1,), (0,)), ((), ())), preferred_element_type=F32)


def dot_t(a, b):
    return lax.dot_general(a, b, (((1,), (1,)), ((), ())), preferred_element_type=F32)


CHUNK = 8


def attention_kernel(place_ref, q_ref, kv_ref, o_ref, q_s, m_s, l_s, acc_s):
    step = pl.program_id(0)
    place = place_ref[0]
    per_group = HEADS // GROUPS
    rows = per_group * ROWS
    keys = CHUNK * ROWS
    factor = HEAD_WIDTH**-0.5 * 1.4426950408889634

    @pl.when(step == 0)
    def _():
        for i in range(HEADS):
            g, a = divmod(i, per_group)
            q_s[g, a * ROWS : (a + 1) * ROWS, :] = q_ref[:, i * HEAD_WIDTH : (i + 1) * HEAD_WIDTH]
        m_s[...] = jnp.full(m_s.shape, hidden_logits, F32)
        l_s[...] = jnp.zeros(l_s.shape, F32)
        acc_s[...] = jnp.zeros(acc_s.shape, F32)

    def update(masked):
        for g in range(GROUPS):
            k = kv_ref[:, g * HEAD_WIDTH : (g + 1) * HEAD_WIDTH]
            v = kv_ref[:, (GROUPS + g) * HEAD_WIDTH : (GROUPS + g + 1) * HEAD_WIDTH]
            s = dot_t(q_s[g], k)
            if masked:
                row = lax.broadcasted_iota(jnp.int32, (rows, keys), 0) & (ROWS - 1)
                col = lax.broadcasted_iota(jnp.int32, (rows, keys), 1) + (step * CHUNK - place) * ROWS
                s = jnp.where(col <= row, s, hidden_logits)
            best = s[:, :ROWS]
            for b in range(1, CHUNK):
                best = jnp.maximum(best, s[:, b * ROWS : (b + 1) * ROWS])
            m_old = m_s[g]
            m_new = jnp.maximum(m_old, jnp.max(best, axis=1, keepdims=True))
            decay = jnp.exp2((m_old - m_new) * factor)
            m_s[g] = m_new
            m_col = m_new[:, :1] * factor
            p = jnp.exp2(s * factor - m_col)
            total = p[:, :ROWS]
            for b in range(1, CHUNK):
                total = total + p[:, b * ROWS : (b + 1) * ROWS]
            l_s[g] = l_s[g] * decay + total
            acc_s[g] = acc_s[g] * decay + dot(p.astype(BF16), v)

    @pl.when((step + 1) * CHUNK <= place)
    def _():
        update(False)

    @pl.when(((step + 1) * CHUNK > place) & (step * CHUNK <= place))
    def _():
        update(True)

    @pl.when(step == pl.num_programs(0) - 1)
    def _():
        for i in range(HEADS):
            g, a = divmod(i, per_group)
            at = slice(a * ROWS, (a + 1) * ROWS)
            total = jnp.sum(l_s[g, at, :], axis=1, keepdims=True)
            o_ref[:, i * HEAD_WIDTH : (i + 1) * HEAD_WIDTH] = (acc_s[g, at, :] / total).astype(BF16)


def attention(place, queries, kv):
    steps = kv.shape[0] // (CHUNK * ROWS)
    rows = HEADS // GROUPS * ROWS
    keys = CHUNK * ROWS
    return pl.pallas_call(
        attention_kernel,
        grid_spec=pltpu.PrefetchScalarGridSpec(
            num_scalar_prefetch=1,
            grid=(steps,),
            in_specs=[
                pl.BlockSpec((ROWS, WIDTH), lambda i, s: (0, 0)),
                pl.BlockSpec((keys, kv.shape[1]), lambda i, s: (jnp.minimum(i, s[0] // CHUNK), 0)),
            ],
            out_specs=pl.BlockSpec((ROWS, WIDTH), lambda i, s: (0, 0)),
            scratch_shapes=[
                pltpu.VMEM((GROUPS, rows, HEAD_WIDTH), BF16),
                pltpu.VMEM((GROUPS, rows, HEAD_WIDTH), F32),
                pltpu.VMEM((GROUPS, rows, HEAD_WIDTH), F32),
                pltpu.VMEM((GROUPS, rows, HEAD_WIDTH), F32),
            ],
        ),
        out_shape=jax.ShapeDtypeStruct((ROWS, WIDTH), BF16),
        compiler_params=params(40),
        name="attention",
    )(place, queries, kv)


def pieces_of(values):
    return [values[:, j * PIECE : (j + 1) * PIECE] for j in range(PIECES)]


def send_kernel(picker_ref, rows_ref, spread_ref, o_ref):
    for b in range(BUNCHES):
        picked = dot(picker_ref[b * COMPACT : (b + 1) * COMPACT, :], rows_ref[...]).astype(BF16)
        out = sum(dot(spread_ref[j], part) for j, part in enumerate(pieces_of(picked)))
        o_ref[b * SPREAD : (b + 1) * SPREAD, :] = out.astype(BF16)


def send_rows(picker, rows, spread):
    return pl.pallas_call(
        send_kernel,
        out_shape=jax.ShapeDtypeStruct((PLACES * PIECES, PIECE), BF16),
        compiler_params=params(14),
        name="send_rows",
    )(picker, rows, spread)


def gather_compact(source_ref, gather_ref, target_ref):
    for b in range(BUNCHES):
        part = source_ref[b * SPREAD : (b + 1) * SPREAD, :]
        for j in range(PIECES):
            target_ref[b * COMPACT : (b + 1) * COMPACT, j * PIECE : (j + 1) * PIECE] = dot(
                gather_ref[j], part
            ).astype(BF16)


TILE = 256


def high_low(x):
    high = x.astype(BF16).astype(F32)
    column = lax.broadcasted_iota(jnp.int32, (x.shape[0], 128), 1)
    return jnp.where(column == 0, high, jnp.where(column == 1, x - high, 0.0)).astype(BF16)


def first_kernel(by_rows, x_ref, gather_ref, w_ref, o_ref, compact_ref, squares_ref):
    @pl.when(pl.program_id(0) == 0)
    def _():
        gather_compact(x_ref, gather_ref, compact_ref)
        for b in range(BUNCHES):
            rows = compact_ref[b * COMPACT : (b + 1) * COMPACT, :].astype(F32)
            squares_ref[b * COMPACT : (b + 1) * COMPACT, :] = high_low(
                jnp.sum(rows * rows, axis=1, keepdims=True)
            )

    product = dot_t if by_rows else dot
    o_ref[...] = product(compact_ref[...], w_ref[...]).astype(BF16)


def first_product(x, gather, w, by_rows):
    if by_rows:
        outs = w.shape[0]
        w_spec = pl.BlockSpec((TILE, WIDTH), lambda i: (i, 0))
    else:
        outs = w.shape[1]
        w_spec = pl.BlockSpec((WIDTH, TILE), lambda i: (0, i))
    return pl.pallas_call(
        functools.partial(first_kernel, by_rows),
        grid=(outs // TILE,),
        in_specs=[
            pl.BlockSpec(x.shape, lambda i: (0, 0)),
            pl.BlockSpec(gather.shape, lambda i: (0, 0, 0)),
            w_spec,
        ],
        out_specs=[
            pl.BlockSpec((PLACES, TILE), lambda i: (0, i)),
            pl.BlockSpec((PLACES, WIDTH), lambda i: (0, 0)),
            pl.BlockSpec((PLACES, 128), lambda i: (0, 0)),
        ],
        out_shape=[
            jax.ShapeDtypeStruct((PLACES, outs), BF16),
            jax.ShapeDtypeStruct((PLACES, WIDTH), BF16),
            jax.ShapeDtypeStruct((PLACES, 128), BF16),
        ],
        compiler_params=params(22),
        name="first_product",
    )(x, gather, w)


def second_kernel(by_rows, corrected, head_ref, *refs):
    pieces, refs = refs[:HEAD_COUNT], refs[HEAD_COUNT:]
    if corrected:
        w_ref, spread_ref, row_ref, o_ref, h_s, y_s, weight_s = refs
    else:
        w_ref, spread_ref, o_ref, h_s, y_s = refs
    step = pl.program_id(0)
    depth = h_s.shape[1]
    quarter = PLACES // HEAD_COUNT

    @pl.when(step == 0)
    def _():
        for d, piece in enumerate(pieces):
            at = lax.rem(head_ref[0] + d, HEAD_COUNT) * quarter
            at = pl.ds(pl.multiple_of(at, 16), quarter)
            h_s[at, :] = piece[:, :depth]
            if corrected:
                weight_s[at, :] = piece[:, depth : depth + 128].astype(F32)

    product = dot_t if by_rows else dot
    y = product(h_s[...], w_ref[...])
    if corrected:
        y = y - row_ref[...].astype(F32) * (weight_s[:, 0:1] + weight_s[:, 1:2])
    y_s[step] = y.astype(BF16)

    @pl.when(step == PIECES - 1)
    def _():
        for b in range(BUNCHES):
            out = sum(
                dot(spread_ref[j], y_s[j, b * COMPACT : (b + 1) * COMPACT, :]) for j in range(PIECES)
            )
            o_ref[b * SPREAD : (b + 1) * SPREAD, :] = out.astype(BF16)


def second_product(head, pieces, w, spread, by_rows, rows=None):
    depth = w.shape[1] if by_rows else w.shape[0]
    w_spec = (
        pl.BlockSpec((PIECE, depth), lambda i, s: (i, 0))
        if by_rows
        else pl.BlockSpec((depth, PIECE), lambda i, s: (0, i))
    )
    in_specs = [pl.BlockSpec(piece.shape, lambda i, s: (0, 0)) for piece in pieces] + [
        w_spec,
        pl.BlockSpec(spread.shape, lambda i, s: (0, 0, 0)),
    ]
    args = [*pieces, w, spread]
    scratch = [pltpu.VMEM((PLACES, depth), BF16), pltpu.VMEM((PIECES, PLACES, PIECE), BF16)]
    if rows is not None:
        in_specs += [pl.BlockSpec((PLACES, PIECE), lambda i, s: (0, i))]
        args += [rows]
        scratch += [pltpu.VMEM((PLACES, 128), F32)]
    return pl.pallas_call(
        functools.partial(second_kernel, by_rows, rows is not None),
        grid_spec=pltpu.PrefetchScalarGridSpec(
            num_scalar_prefetch=1,
            grid=(PIECES,),
            in_specs=in_specs,
            out_specs=pl.BlockSpec((PLACES * PIECES, PIECE), lambda i, s: (0, 0)),
            scratch_shapes=scratch,
        ),
        out_shape=jax.ShapeDtypeStruct((PLACES * PIECES, PIECE), BF16),
        compiler_params=params(32),
        name="second_product",
    )(head[None], *args)


def combine_kernel(came_ref, gather_ref, weight_ref, base_ref, o_ref, compact_s):
    gather_compact(came_ref, gather_ref, compact_s)
    both = dot(weight_ref[...], compact_s[...])
    o_ref[...] = (base_ref[...].astype(F32) + (both[:ROWS] + both[ROWS:])).astype(BF16)


def combine(came, gather, weight, base):
    return pl.pallas_call(
        combine_kernel,
        out_shape=jax.ShapeDtypeStruct((ROWS, WIDTH), BF16),
        scratch_shapes=[pltpu.VMEM((PLACES, WIDTH), BF16)],
        compiler_params=params(18),
        name="combine",
    )(came, gather, weight, base)


def exchange(x):
    y = lax.all_to_all(
        x.reshape(EXPERTS, CAP * PIECES, PIECE), "exp", split_axis=0, concat_axis=0, tiled=True
    )
    return y.reshape(PLACES * PIECES, PIECE)


def from_head(x, d):
    return lax.ppermute(x, "head", [((i + d) % HEAD_COUNT, i) for i in range(HEAD_COUNT)])


OTHERS = (1, 3, 2)


def head_scatter(head, x):
    rows = x.shape[0] // HEAD_COUNT

    def part(d):
        return lax.dynamic_slice_in_dim(x, (head + d) % HEAD_COUNT * rows, rows)

    return [part(0)] + [from_head(part(-d), d) for d in OTHERS]


def head_gather(x):
    parts = {d: from_head(x, d) for d in OTHERS}
    return [x] + [parts[d] for d in range(1, HEAD_COUNT)]


def total(parts):
    return functools.reduce(jnp.add, [part.astype(F32) for part in parts])


def per_device(queries, keys, values, w_in, w_out, routes, route_weights, grad_out):
    place = lax.axis_index("exp").astype(jnp.int32)
    head = lax.axis_index("head").astype(jnp.int32)
    w_first = w_in[0].reshape(WIDTH, 2 * FF)
    w_second = w_out[0]
    matrix = spread_matrix()
    spread = jnp.asarray(matrix, BF16)
    gather = jnp.asarray(matrix.transpose(0, 2, 1), BF16)

    hits = routes[:, :, None] == jnp.arange(EXPERTS, dtype=jnp.int32)
    hit = jnp.any(hits, axis=1)
    earlier = jnp.asarray(np.tril(np.ones((ROWS, ROWS), np.float32), -1), BF16)
    rank = dot(earlier, hit.astype(BF16))
    rank = jnp.where(hit, rank, -1.0)
    token_weight = jnp.sum(jnp.where(hits, route_weights[:, :, None], 0.0), axis=1)
    slots = jnp.arange(CAP, dtype=jnp.int32).astype(F32)
    picker = (rank.T[:, None, :] == slots[None, :, None]).astype(BF16).reshape(PLACES, ROWS)
    weight = jnp.where(rank[:, :, None] == slots, token_weight[:, :, None], 0.0).reshape(ROWS, PLACES)
    weight_high = weight.astype(BF16)
    weight_low = (weight - weight_high.astype(F32)).astype(BF16)
    weight_both = jnp.concatenate([weight_high, weight_low], axis=0)

    kv = lax.all_gather(jnp.concatenate([keys, values], axis=1), "exp", axis=0, tiled=True)
    grads_in = exchange(send_rows(picker, grad_out, spread))
    back, _, _ = first_product(grads_in, gather, w_second, True)
    back = head_scatter(head, back)
    kv, weight_both, *back = lax.optimization_barrier((kv, weight_both, *back))
    attended = attention(place[None], queries, kv)

    rows_in = exchange(send_rows(picker, attended, spread))
    raw, rows, squares = first_product(rows_in, gather, w_first, False)
    raw = head_scatter(head, jnp.concatenate([raw, squares], axis=1))
    raw = total(raw)
    squares = raw[:, 2 * FF : 2 * FF + 1] + raw[:, 2 * FF + 1 : 2 * FF + 2]
    scale = lax.rsqrt(squares / D + norm_eps)
    gate = raw[:, :FF] * scale
    lift = raw[:, FF : 2 * FF] * scale
    sigmoid = jax.nn.sigmoid(gate)
    silu = gate * sigmoid
    act = (silu * lift).astype(BF16)
    gathered = head_gather(act)
    back = total(back)
    grad_gate = (back * lift * sigmoid * (1.0 + gate * (1.0 - sigmoid)) * scale).astype(BF16)
    grad_up = (back * silu * scale).astype(BF16)
    inner = jnp.sum(
        grad_gate.astype(F32) * gate + grad_up.astype(F32) * lift, axis=1, keepdims=True
    )
    correction = high_low(inner * scale / D)
    grad_hidden = jnp.concatenate([grad_gate, grad_up, correction], axis=1)
    grad_hidden, *gathered = lax.optimization_barrier((grad_hidden, *gathered))
    came_out = exchange(second_product(head, gathered, w_second, spread, False))
    grad_hidden = head_gather(grad_hidden)
    came_grad = exchange(second_product(head, grad_hidden, w_first, spread, True, rows))
    output = combine(came_out, gather, weight_both, attended)
    grad_attended = combine(came_grad, gather, weight_both, grad_out)
    return (output, grad_attended)


def solution(mesh):
    in_specs = (
        P("exp", "head"),
        P("exp", "head"),
        P("exp", "head"),
        P("exp", "head", None, None),
        P("exp", None, "head"),
        P("exp", None),
        P("exp", None),
        P("exp", "head"),
    )
    out_specs = (P("exp", "head"), P("exp", "head"))
    return jax.shard_map(
        per_device, mesh=mesh, in_specs=in_specs, out_specs=out_specs, check_vma=False
    )
```

```python
import functools

import jax
import jax.numpy as jnp
import numpy as np
from jax import lax
from jax.experimental import pallas as pl
from jax.experimental.pallas import tpu as pltpu
from jax.sharding import PartitionSpec as P

D = 4096
HEAD_WIDTH = 128
TOP = 6
norm_eps = 1e-05
hidden_logits = -1e30

ROWS = 128
HEADS = 8
GROUPS = 2
WIDTH = 1024
FF = 768
EXPERTS = 64
HEAD_COUNT = 4
CAP = 14
PIECES = 4
PIECE = WIDTH // PIECES
BUNCH = 8
COMPACT = BUNCH * CAP
SPREAD = BUNCH * CAP * PIECES
BUNCHES = EXPERTS // BUNCH
PLACES = EXPERTS * CAP
F32 = jnp.float32
BF16 = jnp.bfloat16
MIB = 1 << 20


def params(mib):
    return pltpu.CompilerParams(vmem_limit_bytes=mib * MIB)


def spread_matrix():
    spread = np.arange(SPREAD)
    compact = np.arange(COMPACT)
    source = spread // (CAP * PIECES) * CAP + spread % CAP
    piece = spread % (CAP * PIECES) // CAP
    same = source[:, None] == compact[None, :]
    return np.stack([same & (piece[:, None] == j) for j in range(PIECES)]).astype(np.float32)


def dot(a, b):
    return lax.dot_general(a, b, (((1,), (0,)), ((), ())), preferred_element_type=F32)


def dot_t(a, b):
    return lax.dot_general(a, b, (((1,), (1,)), ((), ())), preferred_element_type=F32)


CHUNK = 8


def attention_kernel(place_ref, q_ref, kv_ref, o_ref, q_s, m_s, l_s, acc_s):
    step = pl.program_id(0)
    place = place_ref[0]
    per_group = HEADS // GROUPS
    rows = per_group * ROWS
    keys = CHUNK * ROWS
    factor = HEAD_WIDTH**-0.5 * 1.4426950408889634

    @pl.when(step == 0)
    def _():
        for i in range(HEADS):
            g, a = divmod(i, per_group)
            q_s[g, a * ROWS : (a + 1) * ROWS, :] = q_ref[:, i * HEAD_WIDTH : (i + 1) * HEAD_WIDTH]
        m_s[...] = jnp.full(m_s.shape, hidden_logits, F32)
        l_s[...] = jnp.zeros(l_s.shape, F32)
        acc_s[...] = jnp.zeros(acc_s.shape, F32)

    def update(masked):
        for g in range(GROUPS):
            k = kv_ref[:, g * HEAD_WIDTH : (g + 1) * HEAD_WIDTH]
            v = kv_ref[:, (GROUPS + g) * HEAD_WIDTH : (GROUPS + g + 1) * HEAD_WIDTH]
            s = dot_t(q_s[g], k)
            if masked:
                row = lax.broadcasted_iota(jnp.int32, (rows, keys), 0) & (ROWS - 1)
                col = lax.broadcasted_iota(jnp.int32, (rows, keys), 1) + (step * CHUNK - place) * ROWS
                s = jnp.where(col <= row, s, hidden_logits)
            best = s[:, :ROWS]
            for b in range(1, CHUNK):
                best = jnp.maximum(best, s[:, b * ROWS : (b + 1) * ROWS])
            m_old = m_s[g]
            m_new = jnp.maximum(m_old, jnp.max(best, axis=1, keepdims=True))
            decay = jnp.exp2((m_old - m_new) * factor)
            m_s[g] = m_new
            m_col = m_new[:, :1] * factor
            p = jnp.exp2(s * factor - m_col)
            total = p[:, :ROWS]
            for b in range(1, CHUNK):
                total = total + p[:, b * ROWS : (b + 1) * ROWS]
            l_s[g] = l_s[g] * decay + total
            acc_s[g] = acc_s[g] * decay + dot(p.astype(BF16), v)

    @pl.when((step + 1) * CHUNK <= place)
    def _():
        update(False)

    @pl.when(((step + 1) * CHUNK > place) & (step * CHUNK <= place))
    def _():
        update(True)

    @pl.when(step == pl.num_programs(0) - 1)
    def _():
        for i in range(HEADS):
            g, a = divmod(i, per_group)
            at = slice(a * ROWS, (a + 1) * ROWS)
            total = jnp.sum(l_s[g, at, :], axis=1, keepdims=True)
            o_ref[:, i * HEAD_WIDTH : (i + 1) * HEAD_WIDTH] = (acc_s[g, at, :] / total).astype(BF16)


def attention(place, queries, kv):
    steps = kv.shape[0] // (CHUNK * ROWS)
    rows = HEADS // GROUPS * ROWS
    keys = CHUNK * ROWS
    return pl.pallas_call(
        attention_kernel,
        grid_spec=pltpu.PrefetchScalarGridSpec(
            num_scalar_prefetch=1,
            grid=(steps,),
            in_specs=[
                pl.BlockSpec((ROWS, WIDTH), lambda i, s: (0, 0)),
                pl.BlockSpec((keys, kv.shape[1]), lambda i, s: (jnp.minimum(i, s[0] // CHUNK), 0)),
            ],
            out_specs=pl.BlockSpec((ROWS, WIDTH), lambda i, s: (0, 0)),
            scratch_shapes=[
                pltpu.VMEM((GROUPS, rows, HEAD_WIDTH), BF16),
                pltpu.VMEM((GROUPS, rows, HEAD_WIDTH), F32),
                pltpu.VMEM((GROUPS, rows, HEAD_WIDTH), F32),
                pltpu.VMEM((GROUPS, rows, HEAD_WIDTH), F32),
            ],
        ),
        out_shape=jax.ShapeDtypeStruct((ROWS, WIDTH), BF16),
        compiler_params=params(58),
        name="attention",
    )(place, queries, kv)


def pieces_of(values):
    return [values[:, j * PIECE : (j + 1) * PIECE] for j in range(PIECES)]


def send_kernel(picker_ref, rows_ref, spread_ref, o_ref):
    for b in range(BUNCHES):
        picked = dot(picker_ref[b * COMPACT : (b + 1) * COMPACT, :], rows_ref[...]).astype(BF16)
        out = sum(dot(spread_ref[j], part) for j, part in enumerate(pieces_of(picked)))
        o_ref[b * SPREAD : (b + 1) * SPREAD, :] = out.astype(BF16)


def send_rows(picker, rows, spread):
    return pl.pallas_call(
        send_kernel,
        out_shape=jax.ShapeDtypeStruct((PLACES * PIECES, PIECE), BF16),
        compiler_params=params(14),
        name="send_rows",
    )(picker, rows, spread)


def gather_compact(source_ref, gather_ref, target_ref):
    for b in range(BUNCHES):
        part = source_ref[b * SPREAD : (b + 1) * SPREAD, :]
        for j in range(PIECES):
            target_ref[b * COMPACT : (b + 1) * COMPACT, j * PIECE : (j + 1) * PIECE] = dot(
                gather_ref[j], part
            ).astype(BF16)


TILE = 256


def high_low(x):
    high = x.astype(BF16).astype(F32)
    column = lax.broadcasted_iota(jnp.int32, (x.shape[0], 128), 1)
    return jnp.where(column == 0, high, jnp.where(column == 1, x - high, 0.0)).astype(BF16)


def first_kernel(by_rows, x_ref, gather_ref, w_ref, o_ref, compact_ref, squares_ref):
    @pl.when(pl.program_id(0) == 0)
    def _():
        gather_compact(x_ref, gather_ref, compact_ref)
        for b in range(BUNCHES):
            rows = compact_ref[b * COMPACT : (b + 1) * COMPACT, :].astype(F32)
            squares_ref[b * COMPACT : (b + 1) * COMPACT, :] = high_low(
                jnp.sum(rows * rows, axis=1, keepdims=True)
            )

    product = dot_t if by_rows else dot
    o_ref[...] = product(compact_ref[...], w_ref[...]).astype(BF16)


def first_product(x, gather, w, by_rows):
    if by_rows:
        outs = w.shape[0]
        w_spec = pl.BlockSpec((TILE, WIDTH), lambda i: (i, 0))
    else:
        outs = w.shape[1]
        w_spec = pl.BlockSpec((WIDTH, TILE), lambda i: (0, i))
    return pl.pallas_call(
        functools.partial(first_kernel, by_rows),
        grid=(outs // TILE,),
        in_specs=[
            pl.BlockSpec(x.shape, lambda i: (0, 0)),
            pl.BlockSpec(gather.shape, lambda i: (0, 0, 0)),
            w_spec,
        ],
        out_specs=[
            pl.BlockSpec((PLACES, TILE), lambda i: (0, i)),
            pl.BlockSpec((PLACES, WIDTH), lambda i: (0, 0)),
            pl.BlockSpec((PLACES, 128), lambda i: (0, 0)),
        ],
        out_shape=[
            jax.ShapeDtypeStruct((PLACES, outs), BF16),
            jax.ShapeDtypeStruct((PLACES, WIDTH), BF16),
            jax.ShapeDtypeStruct((PLACES, 128), BF16),
        ],
        compiler_params=params(22),
        name="first_product",
    )(x, gather, w)


def second_kernel(by_rows, corrected, head_ref, *refs):
    pieces, refs = refs[:HEAD_COUNT], refs[HEAD_COUNT:]
    if corrected:
        w_ref, spread_ref, row_ref, o_ref, h_s, y_s, weight_s = refs
    else:
        w_ref, spread_ref, o_ref, h_s, y_s = refs
    step = pl.program_id(0)
    depth = h_s.shape[1]
    quarter = PLACES // HEAD_COUNT

    @pl.when(step == 0)
    def _():
        for d, piece in enumerate(pieces):
            at = lax.rem(head_ref[0] + d, HEAD_COUNT) * quarter
            at = pl.ds(pl.multiple_of(at, 16), quarter)
            h_s[at, :] = piece[:, :depth]
            if corrected:
                weight_s[at, :] = piece[:, depth : depth + 128].astype(F32)

    product = dot_t if by_rows else dot
    y = product(h_s[...], w_ref[...])
    if corrected:
        y = y - row_ref[...].astype(F32) * (weight_s[:, 0:1] + weight_s[:, 1:2])
    y_s[step] = y.astype(BF16)

    @pl.when(step == PIECES - 1)
    def _():
        for b in range(BUNCHES):
            out = sum(
                dot(spread_ref[j], y_s[j, b * COMPACT : (b + 1) * COMPACT, :]) for j in range(PIECES)
            )
            o_ref[b * SPREAD : (b + 1) * SPREAD, :] = out.astype(BF16)


def second_product(head, pieces, w, spread, by_rows, rows=None):
    depth = w.shape[1] if by_rows else w.shape[0]
    w_spec = (
        pl.BlockSpec((PIECE, depth), lambda i, s: (i, 0))
        if by_rows
        else pl.BlockSpec((depth, PIECE), lambda i, s: (0, i))
    )
    in_specs = [pl.BlockSpec(piece.shape, lambda i, s: (0, 0)) for piece in pieces] + [
        w_spec,
        pl.BlockSpec(spread.shape, lambda i, s: (0, 0, 0)),
    ]
    args = [*pieces, w, spread]
    scratch = [pltpu.VMEM((PLACES, depth), BF16), pltpu.VMEM((PIECES, PLACES, PIECE), BF16)]
    if rows is not None:
        in_specs += [pl.BlockSpec((PLACES, PIECE), lambda i, s: (0, i))]
        args += [rows]
        scratch += [pltpu.VMEM((PLACES, 128), F32)]
    return pl.pallas_call(
        functools.partial(second_kernel, by_rows, rows is not None),
        grid_spec=pltpu.PrefetchScalarGridSpec(
            num_scalar_prefetch=1,
            grid=(PIECES,),
            in_specs=in_specs,
            out_specs=pl.BlockSpec((PLACES * PIECES, PIECE), lambda i, s: (0, 0)),
            scratch_shapes=scratch,
        ),
        out_shape=jax.ShapeDtypeStruct((PLACES * PIECES, PIECE), BF16),
        compiler_params=params(32),
        name="second_product",
    )(head[None], *args)


def combine_kernel(came_ref, gather_ref, weight_ref, base_ref, o_ref, compact_s):
    gather_compact(came_ref, gather_ref, compact_s)
    both = dot(weight_ref[...], compact_s[...])
    o_ref[...] = (base_ref[...].astype(F32) + (both[:ROWS] + both[ROWS:])).astype(BF16)


def combine(came, gather, weight, base):
    return pl.pallas_call(
        combine_kernel,
        out_shape=jax.ShapeDtypeStruct((ROWS, WIDTH), BF16),
        scratch_shapes=[pltpu.VMEM((PLACES, WIDTH), BF16)],
        compiler_params=params(18),
        name="combine",
    )(came, gather, weight, base)


def exchange(x):
    y = lax.all_to_all(
        x.reshape(EXPERTS, CAP * PIECES, PIECE), "exp", split_axis=0, concat_axis=0, tiled=True
    )
    return y.reshape(PLACES * PIECES, PIECE)


def from_head(x, d):
    return lax.ppermute(x, "head", [((i + d) % HEAD_COUNT, i) for i in range(HEAD_COUNT)])


OTHERS = (1, 3, 2)


def head_scatter(head, x):
    rows = x.shape[0] // HEAD_COUNT

    def part(d):
        return lax.dynamic_slice_in_dim(x, (head + d) % HEAD_COUNT * rows, rows)

    return [part(0)] + [from_head(part(-d), d) for d in OTHERS]


def head_gather(x):
    parts = {d: from_head(x, d) for d in OTHERS}
    return [x] + [parts[d] for d in range(1, HEAD_COUNT)]


def head_gather_twice(x):
    half = x.shape[0] // 2
    low = from_head(x, 3)
    high = from_head(x, 1)
    opposite = jnp.concatenate([from_head(low[:half], 3), from_head(high[half:], 1)])
    return [x, high, opposite, low]


def total(parts):
    return functools.reduce(jnp.add, [part.astype(F32) for part in parts])


def per_device(queries, keys, values, w_in, w_out, routes, route_weights, grad_out):
    place = lax.axis_index("exp").astype(jnp.int32)
    head = lax.axis_index("head").astype(jnp.int32)
    w_first = w_in[0].reshape(WIDTH, 2 * FF)
    w_second = w_out[0]
    matrix = spread_matrix()
    spread = jnp.asarray(matrix, BF16)
    gather = jnp.asarray(matrix.transpose(0, 2, 1), BF16)

    own_kv = jnp.concatenate([keys, values], axis=1)
    own_kv, routes, route_weights = lax.optimization_barrier((own_kv, routes, route_weights))
    kv = lax.all_gather(own_kv, "exp", axis=0, tiled=True)

    hits = routes[:, :, None] == jnp.arange(EXPERTS, dtype=jnp.int32)
    hit = jnp.any(hits, axis=1)
    earlier = jnp.asarray(np.tril(np.ones((ROWS, ROWS), np.float32), -1), BF16)
    rank = dot(earlier, hit.astype(BF16))
    rank = jnp.where(hit, rank, -1.0)
    token_weight = jnp.sum(jnp.where(hits, route_weights[:, :, None], 0.0), axis=1)
    slots = jnp.arange(CAP, dtype=jnp.int32).astype(F32)
    picker = (rank.T[:, None, :] == slots[None, :, None]).astype(BF16).reshape(PLACES, ROWS)
    weight = jnp.where(rank[:, :, None] == slots, token_weight[:, :, None], 0.0).reshape(ROWS, PLACES)
    weight_high = weight.astype(BF16)
    weight_low = (weight - weight_high.astype(F32)).astype(BF16)
    weight_both = jnp.concatenate([weight_high, weight_low], axis=0)

    grads_in = exchange(send_rows(picker, grad_out, spread))
    back, _, _ = first_product(grads_in, gather, w_second, True)
    back = head_scatter(head, back)
    kv, weight_both, *back = lax.optimization_barrier((kv, weight_both, *back))
    attended = attention(place[None], queries, kv)

    rows_in = exchange(send_rows(picker, attended, spread))
    raw, rows, squares = first_product(rows_in, gather, w_first, False)
    raw = head_scatter(head, jnp.concatenate([raw, squares], axis=1))
    raw = total(raw)
    squares = raw[:, 2 * FF : 2 * FF + 1] + raw[:, 2 * FF + 1 : 2 * FF + 2]
    scale = lax.rsqrt(squares / D + norm_eps)
    gate = raw[:, :FF] * scale
    lift = raw[:, FF : 2 * FF] * scale
    sigmoid = jax.nn.sigmoid(gate)
    silu = gate * sigmoid
    act = (silu * lift).astype(BF16)
    gathered = head_gather(act)
    back = total(back)
    grad_gate = (back * lift * sigmoid * (1.0 + gate * (1.0 - sigmoid)) * scale).astype(BF16)
    grad_up = (back * silu * scale).astype(BF16)
    inner = jnp.sum(
        grad_gate.astype(F32) * gate + grad_up.astype(F32) * lift, axis=1, keepdims=True
    )
    correction = high_low(inner * scale / D)
    grad_hidden = jnp.concatenate([grad_gate, grad_up, correction], axis=1)
    grad_hidden, *gathered = lax.optimization_barrier((grad_hidden, *gathered))
    came_out = exchange(second_product(head, gathered, w_second, spread, False))
    grad_hidden = head_gather_twice(grad_hidden)
    came_grad = exchange(second_product(head, grad_hidden, w_first, spread, True, rows))
    output = combine(came_out, gather, weight_both, attended)
    grad_attended = combine(came_grad, gather, weight_both, grad_out)
    return (output, grad_attended)


def solution(mesh):
    in_specs = (
        P("exp", "head"),
        P("exp", "head"),
        P("exp", "head"),
        P("exp", "head", None, None),
        P("exp", None, "head"),
        P("exp", None),
        P("exp", None),
        P("exp", "head"),
    )
    out_specs = (P("exp", "head"), P("exp", "head"))
    return jax.shard_map(
        per_device, mesh=mesh, in_specs=in_specs, out_specs=out_specs, check_vma=False
    )
```

```python
import functools

import jax
import jax.numpy as jnp
import numpy as np
from jax import lax
from jax.experimental import pallas as pl
from jax.experimental.pallas import tpu as pltpu
from jax.sharding import PartitionSpec as P

D = 4096
HEAD_WIDTH = 128
TOP = 6
norm_eps = 1e-05
hidden_logits = -1e30

ROWS = 128
HEADS = 8
GROUPS = 2
WIDTH = 1024
FF = 768
EXPERTS = 64
HEAD_COUNT = 4
CAP = 14
PIECES = 4
PIECE = WIDTH // PIECES
BUNCH = 8
COMPACT = BUNCH * CAP
SPREAD = BUNCH * CAP * PIECES
BUNCHES = EXPERTS // BUNCH
PLACES = EXPERTS * CAP
F32 = jnp.float32
BF16 = jnp.bfloat16
MIB = 1 << 20


def params(mib):
    return pltpu.CompilerParams(vmem_limit_bytes=mib * MIB)


def spread_matrix():
    spread = np.arange(SPREAD)
    compact = np.arange(COMPACT)
    source = spread // (CAP * PIECES) * CAP + spread % CAP
    piece = spread % (CAP * PIECES) // CAP
    same = source[:, None] == compact[None, :]
    return np.stack([same & (piece[:, None] == j) for j in range(PIECES)]).astype(np.float32)


def dot(a, b):
    return lax.dot_general(a, b, (((1,), (0,)), ((), ())), preferred_element_type=F32)


def dot_t(a, b):
    return lax.dot_general(a, b, (((1,), (1,)), ((), ())), preferred_element_type=F32)


CHUNK = 16


def attention_kernel(place_ref, q_ref, kv_ref, o_ref, q_s, m_s, l_s, acc_s):
    step = pl.program_id(0)
    place = place_ref[0]
    per_group = HEADS // GROUPS
    rows = per_group * ROWS
    keys = CHUNK * ROWS
    factor = HEAD_WIDTH**-0.5 * 1.4426950408889634

    @pl.when(step == 0)
    def _():
        for i in range(HEADS):
            g, a = divmod(i, per_group)
            q_s[g, a * ROWS : (a + 1) * ROWS, :] = q_ref[:, i * HEAD_WIDTH : (i + 1) * HEAD_WIDTH]
        m_s[...] = jnp.full(m_s.shape, hidden_logits, F32)
        l_s[...] = jnp.zeros(l_s.shape, F32)
        acc_s[...] = jnp.zeros(acc_s.shape, F32)

    def update(masked):
        for g in range(GROUPS):
            k = kv_ref[:, g * HEAD_WIDTH : (g + 1) * HEAD_WIDTH]
            v = kv_ref[:, (GROUPS + g) * HEAD_WIDTH : (GROUPS + g + 1) * HEAD_WIDTH]
            s = dot_t(q_s[g], k)
            if masked:
                row = lax.broadcasted_iota(jnp.int32, (rows, keys), 0) & (ROWS - 1)
                col = lax.broadcasted_iota(jnp.int32, (rows, keys), 1) + (step * CHUNK - place) * ROWS
                s = jnp.where(col <= row, s, hidden_logits)
            best = s[:, :ROWS]
            for b in range(1, CHUNK):
                best = jnp.maximum(best, s[:, b * ROWS : (b + 1) * ROWS])
            m_old = m_s[g]
            m_new = jnp.maximum(m_old, jnp.max(best, axis=1, keepdims=True))
            decay = jnp.exp2((m_old - m_new) * factor)
            m_s[g] = m_new
            m_col = m_new[:, :1] * factor
            p = jnp.exp2(s * factor - m_col)
            total = p[:, :ROWS]
            for b in range(1, CHUNK):
                total = total + p[:, b * ROWS : (b + 1) * ROWS]
            l_s[g] = l_s[g] * decay + total
            acc_s[g] = acc_s[g] * decay + dot(p.astype(BF16), v)

    @pl.when((step + 1) * CHUNK <= place)
    def _():
        update(False)

    @pl.when(((step + 1) * CHUNK > place) & (step * CHUNK <= place))
    def _():
        update(True)

    @pl.when(step == pl.num_programs(0) - 1)
    def _():
        for i in range(HEADS):
            g, a = divmod(i, per_group)
            at = slice(a * ROWS, (a + 1) * ROWS)
            total = jnp.sum(l_s[g, at, :], axis=1, keepdims=True)
            o_ref[:, i * HEAD_WIDTH : (i + 1) * HEAD_WIDTH] = (acc_s[g, at, :] / total).astype(BF16)


def attention(place, queries, kv):
    steps = kv.shape[0] // (CHUNK * ROWS)
    rows = HEADS // GROUPS * ROWS
    keys = CHUNK * ROWS
    return pl.pallas_call(
        attention_kernel,
        grid_spec=pltpu.PrefetchScalarGridSpec(
            num_scalar_prefetch=1,
            grid=(steps,),
            in_specs=[
                pl.BlockSpec((ROWS, WIDTH), lambda i, s: (0, 0)),
                pl.BlockSpec((keys, kv.shape[1]), lambda i, s: (jnp.minimum(i, s[0] // CHUNK), 0)),
            ],
            out_specs=pl.BlockSpec((ROWS, WIDTH), lambda i, s: (0, 0)),
            scratch_shapes=[
                pltpu.VMEM((GROUPS, rows, HEAD_WIDTH), BF16),
                pltpu.VMEM((GROUPS, rows, HEAD_WIDTH), F32),
                pltpu.VMEM((GROUPS, rows, HEAD_WIDTH), F32),
                pltpu.VMEM((GROUPS, rows, HEAD_WIDTH), F32),
            ],
        ),
        out_shape=jax.ShapeDtypeStruct((ROWS, WIDTH), BF16),
        compiler_params=params(58),
        name="attention",
    )(place, queries, kv)


def pieces_of(values):
    return [values[:, j * PIECE : (j + 1) * PIECE] for j in range(PIECES)]


def send_kernel(picker_ref, rows_ref, spread_ref, o_ref):
    for b in range(BUNCHES):
        picked = dot(picker_ref[b * COMPACT : (b + 1) * COMPACT, :], rows_ref[...]).astype(BF16)
        out = sum(dot(spread_ref[j], part) for j, part in enumerate(pieces_of(picked)))
        o_ref[b * SPREAD : (b + 1) * SPREAD, :] = out.astype(BF16)


def send_rows(picker, rows, spread):
    return pl.pallas_call(
        send_kernel,
        out_shape=jax.ShapeDtypeStruct((PLACES * PIECES, PIECE), BF16),
        compiler_params=params(14),
        name="send_rows",
    )(picker, rows, spread)


def gather_compact(source_ref, gather_ref, target_ref):
    for b in range(BUNCHES):
        part = source_ref[b * SPREAD : (b + 1) * SPREAD, :]
        for j in range(PIECES):
            target_ref[b * COMPACT : (b + 1) * COMPACT, j * PIECE : (j + 1) * PIECE] = dot(
                gather_ref[j], part
            ).astype(BF16)


TILE = 768


def high_low(x):
    high = x.astype(BF16).astype(F32)
    column = lax.broadcasted_iota(jnp.int32, (x.shape[0], 128), 1)
    return jnp.where(column == 0, high, jnp.where(column == 1, x - high, 0.0)).astype(BF16)


def first_kernel(by_rows, x_ref, gather_ref, w_ref, o_ref, compact_ref, squares_ref):
    @pl.when(pl.program_id(0) == 0)
    def _():
        gather_compact(x_ref, gather_ref, compact_ref)
        for b in range(BUNCHES):
            rows = compact_ref[b * COMPACT : (b + 1) * COMPACT, :].astype(F32)
            squares_ref[b * COMPACT : (b + 1) * COMPACT, :] = high_low(
                jnp.sum(rows * rows, axis=1, keepdims=True)
            )

    product = dot_t if by_rows else dot
    o_ref[...] = product(compact_ref[...], w_ref[...]).astype(BF16)


def first_product(x, gather, w, by_rows):
    if by_rows:
        outs = w.shape[0]
        w_spec = pl.BlockSpec((TILE, WIDTH), lambda i: (i, 0))
    else:
        outs = w.shape[1]
        w_spec = pl.BlockSpec((WIDTH, TILE), lambda i: (0, i))
    return pl.pallas_call(
        functools.partial(first_kernel, by_rows),
        grid=(outs // TILE,),
        in_specs=[
            pl.BlockSpec(x.shape, lambda i: (0, 0)),
            pl.BlockSpec(gather.shape, lambda i: (0, 0, 0)),
            w_spec,
        ],
        out_specs=[
            pl.BlockSpec((PLACES, TILE), lambda i: (0, i)),
            pl.BlockSpec((PLACES, WIDTH), lambda i: (0, 0)),
            pl.BlockSpec((PLACES, 128), lambda i: (0, 0)),
        ],
        out_shape=[
            jax.ShapeDtypeStruct((PLACES, outs), BF16),
            jax.ShapeDtypeStruct((PLACES, WIDTH), BF16),
            jax.ShapeDtypeStruct((PLACES, 128), BF16),
        ],
        compiler_params=params(30),
        name="first_product",
    )(x, gather, w)


def second_kernel(by_rows, corrected, head_ref, *refs):
    pieces, refs = refs[:HEAD_COUNT], refs[HEAD_COUNT:]
    if corrected:
        w_ref, spread_ref, row_ref, o_ref, h_s, y_s, weight_s = refs
    else:
        w_ref, spread_ref, o_ref, h_s, y_s = refs
    step = pl.program_id(0)
    depth = h_s.shape[1]
    quarter = PLACES // HEAD_COUNT

    @pl.when(step == 0)
    def _():
        for d, piece in enumerate(pieces):
            at = lax.rem(head_ref[0] + d, HEAD_COUNT) * quarter
            at = pl.ds(pl.multiple_of(at, 16), quarter)
            h_s[at, :] = piece[:, :depth]
            if corrected:
                weight_s[at, :] = piece[:, depth : depth + 128].astype(F32)

    product = dot_t if by_rows else dot
    y = product(h_s[...], w_ref[...])
    if corrected:
        y = y - row_ref[...].astype(F32) * (weight_s[:, 0:1] + weight_s[:, 1:2])
    y_s[step] = y.astype(BF16)

    @pl.when(step == PIECES - 1)
    def _():
        for b in range(BUNCHES):
            out = sum(
                dot(spread_ref[j], y_s[j, b * COMPACT : (b + 1) * COMPACT, :]) for j in range(PIECES)
            )
            o_ref[b * SPREAD : (b + 1) * SPREAD, :] = out.astype(BF16)


def second_product(head, pieces, w, spread, by_rows, rows=None):
    depth = w.shape[1] if by_rows else w.shape[0]
    w_spec = (
        pl.BlockSpec((PIECE, depth), lambda i, s: (i, 0))
        if by_rows
        else pl.BlockSpec((depth, PIECE), lambda i, s: (0, i))
    )
    in_specs = [pl.BlockSpec(piece.shape, lambda i, s: (0, 0)) for piece in pieces] + [
        w_spec,
        pl.BlockSpec(spread.shape, lambda i, s: (0, 0, 0)),
    ]
    args = [*pieces, w, spread]
    scratch = [pltpu.VMEM((PLACES, depth), BF16), pltpu.VMEM((PIECES, PLACES, PIECE), BF16)]
    if rows is not None:
        in_specs += [pl.BlockSpec((PLACES, PIECE), lambda i, s: (0, i))]
        args += [rows]
        scratch += [pltpu.VMEM((PLACES, 128), F32)]
    return pl.pallas_call(
        functools.partial(second_kernel, by_rows, rows is not None),
        grid_spec=pltpu.PrefetchScalarGridSpec(
            num_scalar_prefetch=1,
            grid=(PIECES,),
            in_specs=in_specs,
            out_specs=pl.BlockSpec((PLACES * PIECES, PIECE), lambda i, s: (0, 0)),
            scratch_shapes=scratch,
        ),
        out_shape=jax.ShapeDtypeStruct((PLACES * PIECES, PIECE), BF16),
        compiler_params=params(32),
        name="second_product",
    )(head[None], *args)


def combine_kernel(came_ref, gather_ref, weight_ref, base_ref, o_ref, compact_s):
    gather_compact(came_ref, gather_ref, compact_s)
    both = dot(weight_ref[...], compact_s[...])
    o_ref[...] = (base_ref[...].astype(F32) + (both[:ROWS] + both[ROWS:])).astype(BF16)


def combine(came, gather, weight, base):
    return pl.pallas_call(
        combine_kernel,
        out_shape=jax.ShapeDtypeStruct((ROWS, WIDTH), BF16),
        scratch_shapes=[pltpu.VMEM((PLACES, WIDTH), BF16)],
        compiler_params=params(18),
        name="combine",
    )(came, gather, weight, base)


def exchange(x):
    y = lax.all_to_all(
        x.reshape(EXPERTS, CAP * PIECES, PIECE), "exp", split_axis=0, concat_axis=0, tiled=True
    )
    return y.reshape(PLACES * PIECES, PIECE)


def from_head(x, d):
    return lax.ppermute(x, "head", [((i + d) % HEAD_COUNT, i) for i in range(HEAD_COUNT)])


OTHERS = (1, 3, 2)


def head_scatter(head, x):
    rows = x.shape[0] // HEAD_COUNT

    def part(d):
        return lax.dynamic_slice_in_dim(x, (head + d) % HEAD_COUNT * rows, rows)

    return [part(0)] + [from_head(part(-d), d) for d in OTHERS]


def head_gather(x):
    parts = {d: from_head(x, d) for d in OTHERS}
    return [x] + [parts[d] for d in range(1, HEAD_COUNT)]


def head_gather_twice(x):
    half = x.shape[0] // 2
    low = from_head(x, 3)
    high = from_head(x, 1)
    opposite = jnp.concatenate([from_head(low[:half], 3), from_head(high[half:], 1)])
    return [x, high, opposite, low]


def total(parts):
    return functools.reduce(jnp.add, [part.astype(F32) for part in parts])


def per_device(queries, keys, values, w_in, w_out, routes, route_weights, grad_out):
    place = lax.axis_index("exp").astype(jnp.int32)
    head = lax.axis_index("head").astype(jnp.int32)
    w_first = w_in[0].reshape(WIDTH, 2 * FF)
    w_second = w_out[0]
    matrix = spread_matrix()
    spread = jnp.asarray(matrix, BF16)
    gather = jnp.asarray(matrix.transpose(0, 2, 1), BF16)

    own_kv = jnp.concatenate([keys, values], axis=1)
    own_kv, routes, route_weights = lax.optimization_barrier((own_kv, routes, route_weights))
    kv = lax.all_gather(own_kv, "exp", axis=0, tiled=True)

    hits = routes[:, :, None] == jnp.arange(EXPERTS, dtype=jnp.int32)
    hit = jnp.any(hits, axis=1)
    earlier = jnp.asarray(np.tril(np.ones((ROWS, ROWS), np.float32), -1), BF16)
    rank = dot(earlier, hit.astype(BF16))
    rank = jnp.where(hit, rank, -1.0)
    token_weight = jnp.sum(jnp.where(hits, route_weights[:, :, None], 0.0), axis=1)
    slots = jnp.arange(CAP, dtype=jnp.int32).astype(F32)
    picker = (rank.T[:, None, :] == slots[None, :, None]).astype(BF16).reshape(PLACES, ROWS)
    weight = jnp.where(rank[:, :, None] == slots, token_weight[:, :, None], 0.0).reshape(ROWS, PLACES)
    weight_high = weight.astype(BF16)
    weight_low = (weight - weight_high.astype(F32)).astype(BF16)
    weight_both = jnp.concatenate([weight_high, weight_low], axis=0)

    grads_in = exchange(send_rows(picker, grad_out, spread))
    back, _, _ = first_product(grads_in, gather, w_second, True)
    back = head_scatter(head, back)
    kv, weight_both, *back = lax.optimization_barrier((kv, weight_both, *back))
    attended = attention(place[None], queries, kv)

    rows_in = exchange(send_rows(picker, attended, spread))
    raw, rows, squares = first_product(rows_in, gather, w_first, False)
    raw = head_scatter(head, jnp.concatenate([raw, squares], axis=1))
    raw = total(raw)
    squares = raw[:, 2 * FF : 2 * FF + 1] + raw[:, 2 * FF + 1 : 2 * FF + 2]
    scale = lax.rsqrt(squares / D + norm_eps)
    gate = raw[:, :FF] * scale
    lift = raw[:, FF : 2 * FF] * scale
    sigmoid = jax.nn.sigmoid(gate)
    silu = gate * sigmoid
    act = (silu * lift).astype(BF16)
    gathered = head_gather(act)
    back = total(back)
    grad_gate = (back * lift * sigmoid * (1.0 + gate * (1.0 - sigmoid)) * scale).astype(BF16)
    grad_up = (back * silu * scale).astype(BF16)
    inner = jnp.sum(
        grad_gate.astype(F32) * gate + grad_up.astype(F32) * lift, axis=1, keepdims=True
    )
    correction = high_low(inner * scale / D)
    grad_hidden = jnp.concatenate([grad_gate, grad_up, correction], axis=1)
    grad_hidden, *gathered = lax.optimization_barrier((grad_hidden, *gathered))
    came_out = exchange(second_product(head, gathered, w_second, spread, False))
    grad_hidden = head_gather_twice(grad_hidden)
    came_grad = exchange(second_product(head, grad_hidden, w_first, spread, True, rows))
    output = combine(came_out, gather, weight_both, attended)
    grad_attended = combine(came_grad, gather, weight_both, grad_out)
    return (output, grad_attended)


def solution(mesh):
    in_specs = (
        P("exp", "head"),
        P("exp", "head"),
        P("exp", "head"),
        P("exp", "head", None, None),
        P("exp", None, "head"),
        P("exp", None),
        P("exp", None),
        P("exp", "head"),
    )
    out_specs = (P("exp", "head"), P("exp", "head"))
    return jax.shard_map(
        per_device, mesh=mesh, in_specs=in_specs, out_specs=out_specs, check_vma=False
    )
```
